512 devices in a mesh: gx: 2 (over y_hi), gy: 16 (over x, y_lo, core), gz: 16 (over z).
Axes of the slice: x: 4, y: 4 (y_hi: 2, y_lo: 2; y = y_hi * 2 + y_lo), z: 16, core: 2. Of those that a mesh axis runs over, the one named last changes fastest.
Arguments:
- positions: float32 [3, 32768], P(None, ('gx', 'gy', 'gz')), may hold values from 0 to 12, as said below
- species: int32 [32768], P(('gx', 'gy', 'gz')), may hold values from 0 to 88
- neighbors: int32 [32768, 64], P(('gx', 'gy', 'gz')), may hold values from 0 to 511, as said below
- neighbor_counts: int32 [32768], P(('gx', 'gy', 'gz')), may hold values from 1 to 64, as said below
- embedding: float32 [89, 128], replicated, may hold values from -6 to 6
- first_inner: float32 [8, 64], replicated, may hold values from -12 to 12
- first_outer: float32 [64, 256], replicated, may hold values from -0.75 to 0.75
- first_scalar: float32 [128, 128], replicated, may hold values from -0.5 to 0.5
- first_vector: float32 [128, 128], replicated, may hold values from -0.5 to 0.5
- first_square: float32 [128, 128], replicated, may hold values from -0.5 to 0.5
- second_inner: float32 [8, 64], replicated, may hold values from -12 to 12
- second_outer: float32 [64, 256], replicated, may hold values from -0.75 to 0.75
- second_mix: float32 [128, 128], replicated, may hold values from -0.5 to 0.5
- readout_first: float32 [128], replicated, may hold values from -0.5 to 0.5
- readout_second: float32 [128], replicated, may hold values from -0.5 to 0.5
Outputs:
- energies: float32 [32768], P(('gx', 'gy', 'gz'))
- forces: float32 [3, 32768], P(None, ('gx', 'gy', 'gz'))
The draws below stay inside these ranges and needn't reach their ends.
Inputs may be any that keep to these rules, and one draw needn't show every extreme that they name: `positions`: atom n of a device lies in [6a, 6a + 6) x [6b, 6b + 6) x [6c, 6c + 6) with 4a + 2b + c = n // 8. `neighbors`: entries index the atom's extended set. `neighbor_counts`: every device has an atom with 64 live slots.
All inputs are finite; a program needn't handle non-finite values.
Results may differ from the reference program's by a relative error of at most 0.0003.
Values sent between devices are 32-bit elements; how exact they have to be, the bound alone decides.
No kernel may reach another device: no remote copies, remote signals or barrier semaphores. Data moves between devices by JAX's collectives and lax.ppermute only.
A program may use at most 64 MiB of HBM per device.

```python
import jax
import jax.numpy as jnp
from jax import lax

C = 128
HID = 64
NB = 8
NSPEC = 89
K = 64
G = 8
ATOMS = 32768
N_GX = 2
N_GY = 16
N_GZ = 16


def draw_positions(key, part):
    key = jax.random.fold_in(key, 11)
    local_index = jnp.arange(ATOMS, dtype=jnp.int32) % (8 * G)
    octant = local_index // G
    octant_bits = jnp.stack([octant // 4, octant // 2 % 2, octant % 2]).astype(jnp.float32)
    fraction = jax.random.uniform(key, (3, ATOMS), jnp.float32, 0.0, 0.999)
    return (octant_bits + fraction) * 6.0


def draw_neighbors(key, part):
    key = jax.random.fold_in(key, 23)
    step_key, slot_key = jax.random.split(key)
    local_index = jnp.arange(ATOMS, dtype=jnp.int32) % (8 * G)
    octant = (local_index // G)[:, None]
    block_steps = jax.random.randint(step_key, (3, ATOMS, K), 0, 3)
    slot_pick = jax.random.randint(slot_key, (ATOMS, K), 0, G)
    along_x = octant // 4 + block_steps[0]
    along_y = octant // 2 % 2 + block_steps[1]
    along_z = octant % 2 + block_steps[2]
    return (((along_x * 4 + along_y) * 4 + along_z) * G + slot_pick).astype(jnp.int32)


def draw_neighbor_counts(key, part):
    key = jax.random.fold_in(key, 37)
    first_key, second_key = jax.random.split(key)
    device_count = ATOMS // (8 * G)
    local_index = jnp.arange(ATOMS, dtype=jnp.int32) % (8 * G)
    device = jnp.arange(ATOMS, dtype=jnp.int32) // (8 * G)
    shortfall = jax.random.randint(first_key, (device_count,), 0, 3 * K // 4)
    missing = jax.random.randint(second_key, (ATOMS,), 0, shortfall[device] + 1)
    return jnp.where(local_index == 0, K, K - missing).astype(jnp.int32)


def touch_ends(values, key, low, largest):
    index_at = [jax.random.randint(jax.random.fold_in(key, axis), (), 0, length) for axis, length in enumerate(values.shape)]
    longest = values.shape.index(max(values.shape))
    beside = index_at[:longest] + [(index_at[longest] + 1) % values.shape[longest]] + index_at[longest + 1:]
    return values.at[tuple(index_at)].set(low).at[tuple(beside)].set(largest)


def gaussian(key, extent, scale, most, held_as=jnp.bfloat16):
    values = jax.random.normal(key, extent, jnp.float32) * scale
    return jnp.minimum(jnp.maximum(values, -most), most).astype(held_as)


def setup_inputs(seed: int = 0) -> dict:
    key_list = jax.random.split(jax.random.key(seed), 16)
    return {
        "positions": draw_positions(jax.random.fold_in(key_list[15], 71), 0),
        "species": touch_ends(jax.random.randint(key_list[1], (ATOMS,), 0, NSPEC), jax.random.fold_in(key_list[1], 1), 0, NSPEC - 1).astype(jnp.int32),
        "neighbors": draw_neighbors(jax.random.fold_in(key_list[15], 71), 0),
        "neighbor_counts": draw_neighbor_counts(jax.random.fold_in(key_list[15], 71), 0),
        "embedding": gaussian(key_list[4], (NSPEC, C), 1.0, 6.0, jnp.float32),
        "first_inner": gaussian(key_list[5], (NB, HID), 2.0, 12.0, jnp.float32),
        "first_outer": gaussian(key_list[6], (HID, 2 * C), HID ** -0.5, 0.75, jnp.float32),
        "first_scalar": gaussian(key_list[7], (C, C), C ** -0.5, 0.5, jnp.float32),
        "first_vector": gaussian(key_list[8], (C, C), C ** -0.5, 0.5, jnp.float32),
        "first_square": gaussian(key_list[9], (C, C), C ** -0.5, 0.5, jnp.float32),
        "second_inner": gaussian(key_list[10], (NB, HID), 2.0, 12.0, jnp.float32),
        "second_outer": gaussian(key_list[11], (HID, 2 * C), HID ** -0.5, 0.75, jnp.float32),
        "second_mix": gaussian(key_list[12], (C, C), C ** -0.5, 0.5, jnp.float32),
        "readout_first": gaussian(key_list[13], (C,), C ** -0.5, 0.5, jnp.float32),
        "readout_second": gaussian(key_list[14], (C,), C ** -0.5, 0.5, jnp.float32),
    }


cutoff = 6.0
box_edge = 12.0
softening = 0.25
message_scale = 0.25
block_atoms = 16
highest = lax.Precision.HIGHEST

def envelope(distance):
    scaled = distance / cutoff
    inside = 1.0 - 28.0 * scaled ** 6 + 48.0 * scaled ** 7 - 21.0 * scaled ** 8
    return jnp.where(scaled < 1.0, inside, 0.0)

def radial(distance, inner, outer):
    orders = jnp.arange(1, inner.shape[0] + 1).astype(jnp.float32)
    angles = jnp.pi / cutoff * distance[..., None] * orders
    bessel = jnp.sqrt(2.0 / cutoff) * jnp.sin(angles) / distance[..., None]
    bessel = bessel * envelope(distance)[..., None]
    hidden = jax.nn.silu(jnp.einsum('akn,nh->akh', bessel, inner, precision=highest))
    return jnp.einsum('akh,hc->akc', hidden, outer, precision=highest)

def geometry(ext_pos, own_pos, neighbor_ids):
    neighbor_pos = jnp.take(ext_pos, neighbor_ids, axis=1)
    separation = neighbor_pos - own_pos[:, :, None]
    distance = jnp.sqrt(lax.optimization_barrier(jnp.sum(separation * separation, axis=0)) + softening)
    return (separation / distance, distance)

def layer_one_block(ext_pos, ext_node, own_pos, own_node, neighbor_ids, live_mask, params):
    inner, outer, mix_scalar, mix_vector, mix_square = params
    channels = own_node.shape[1]
    unit_vec, distance = geometry(ext_pos, own_pos, neighbor_ids)
    weights = radial(distance, inner, outer) * live_mask[..., None]
    sender = jnp.take(ext_node, neighbor_ids, axis=0)
    scalar_msg = message_scale * lax.optimization_barrier(jnp.sum(weights[..., :channels] * sender, axis=1))
    vector_msg = message_scale * jnp.einsum('xak,akc->xac', unit_vec, weights[..., channels:] * sender, precision=highest)
    vector_out = jnp.einsum('xac,cd->xad', vector_msg, mix_vector, precision=highest)
    square = lax.optimization_barrier(jnp.sum(vector_out * vector_out, axis=0))
    scalar_out = jax.nn.silu(jnp.dot(scalar_msg + own_node, mix_scalar, precision=highest) + jnp.dot(square, mix_square, precision=highest))
    return jnp.concatenate([scalar_out, vector_out[0], vector_out[1], vector_out[2]], axis=1)

def layer_two_block(ext_pos, ext_feat, own_pos, own_feat, neighbor_ids, live_mask, params):
    inner, outer, mix_two, read_one, read_two = params
    channels = own_feat.shape[1] // 4
    unit_vec, distance = geometry(ext_pos, own_pos, neighbor_ids)
    weights = radial(distance, inner, outer) * live_mask[..., None]
    sender = jnp.take(ext_feat, neighbor_ids, axis=0)
    projected = unit_vec[0][..., None] * sender[..., channels:2 * channels]
    projected = projected + unit_vec[1][..., None] * sender[..., 2 * channels:3 * channels]
    projected = projected + unit_vec[2][..., None] * sender[..., 3 * channels:]
    message = message_scale * lax.optimization_barrier(jnp.sum(weights[..., :channels] * sender[..., :channels] + weights[..., channels:] * projected, axis=1))
    own_scalar = own_feat[:, :channels]
    hidden = jax.nn.silu(jnp.dot(message + own_scalar, mix_two, precision=highest))
    return jnp.dot(hidden, read_two, precision=highest) + jnp.dot(own_scalar, read_one, precision=highest)

def over_blocks(block_fn, ext_first, ext_second, own_pos, own_feat, neighbor_ids, neighbor_counts, params):
    atom_count, slot_count = neighbor_ids.shape
    block_count = atom_count // block_atoms
    live_mask = (jnp.arange(slot_count, dtype=jnp.int32)[None, :] < neighbor_counts[:, None]).astype(jnp.float32)
    checked = jax.checkpoint(block_fn)

    def one_block(block_item):
        pos_block, feat_block, id_block, mask_block = block_item
        return checked(ext_first, ext_second, pos_block, feat_block, id_block, mask_block, params)
    result = lax.map(one_block, (jnp.moveaxis(own_pos.reshape(3, block_count, block_atoms), 1, 0), own_feat.reshape(block_count, block_atoms, own_feat.shape[1]), neighbor_ids.reshape(block_count, block_atoms, slot_count), live_mask.reshape(block_count, block_atoms, slot_count)))
    return result.reshape((atom_count,) + result.shape[2:])

def offsets():
    shift_values = jnp.array([-box_edge, 0.0, 0.0, box_edge], dtype=jnp.float32)
    return jnp.stack(jnp.broadcast_arrays(shift_values[:, None, None], shift_values[None, :, None], shift_values[None, None, :]), axis=-1)

def grid_index(index_x, index_y, index_z):
    device_step = jnp.array([-1, 0, 0, 1], dtype=jnp.int32)
    block_half = jnp.array([1, 0, 1, 0], dtype=jnp.int32)
    along_x = ((index_x + device_step) % N_GX)[:, None, None]
    along_y = ((index_y + device_step) % N_GY)[None, :, None]
    along_z = ((index_z + device_step) % N_GZ)[None, None, :]
    return (along_x, along_y, along_z, block_half[:, None, None], block_half[None, :, None], block_half[None, None, :])

def grid_take(grid, index_x, index_y, index_z):
    return grid[grid_index(index_x, index_y, index_z)]

def grid_add(grid, index_x, index_y, index_z, extended):
    return grid.at[grid_index(index_x, index_y, index_z)].add(extended)

def reference(positions, species, neighbors, neighbor_counts, embedding, first_inner, first_outer, first_scalar, first_vector, first_square, second_inner, second_outer, second_mix, readout_first, readout_second):
    atoms_dev = 8 * G
    ext_count = 64 * G
    device_total = N_GX * N_GY * N_GZ
    channels = embedding.shape[1]
    grid_shape = (N_GX, N_GY, N_GZ, 2, 2, 2, G)
    pos_grid = jnp.moveaxis(positions.reshape((3,) + grid_shape), 0, -1)
    onehot = (species[:, None] == jnp.arange(NSPEC, dtype=jnp.int32)[None, :]).astype(jnp.float32)
    node_all = jnp.dot(onehot, embedding, precision=highest)
    node_grid = node_all.reshape(grid_shape + (channels,))
    shifts = offsets()
    params_one = (first_inner, first_outer, first_scalar, first_vector, first_square)
    params_two = (second_inner, second_outer, second_mix, readout_first, readout_second)

    def coords(device):
        return (device // (N_GY * N_GZ), device // N_GZ % N_GY, device % N_GZ)

    def rows_of(array, device):
        return lax.dynamic_slice_in_dim(array, device * atoms_dev, atoms_dev, 0)

    def device_inputs(device):
        index_x, index_y, index_z = coords(device)
        ext_pos = (grid_take(pos_grid, index_x, index_y, index_z) + shifts[:, :, :, None, :]).reshape(ext_count, 3).T
        ext_node = grid_take(node_grid, index_x, index_y, index_z).reshape(ext_count, channels)
        own_pos = lax.dynamic_slice_in_dim(positions, device * atoms_dev, atoms_dev, 1)
        return (index_x, index_y, index_z, ext_pos, ext_node, own_pos)

    def first_pass(device):
        index_x, index_y, index_z, ext_pos, ext_node, own_pos = device_inputs(device)
        return over_blocks(layer_one_block, ext_pos, ext_node, own_pos, rows_of(node_all, device), rows_of(neighbors, device), rows_of(neighbor_counts, device), params_one)
    device_ids = jnp.arange(device_total, dtype=jnp.int32)
    features = lax.map(first_pass, device_ids)
    feat_grid = features.reshape(grid_shape + (4 * channels,))

    def second(carry, device):
        feat_acc, pos_acc = carry
        index_x, index_y, index_z, ext_pos, ext_node, own_pos = device_inputs(device)
        ext_feat = grid_take(feat_grid, index_x, index_y, index_z).reshape(ext_count, 4 * channels)
        neighbor_ids = rows_of(neighbors, device)
        counts_dev = rows_of(neighbor_counts, device)

        def energy_fn(ext_position, ext_feature, own_position, own_feature):
            return over_blocks(layer_two_block, ext_position, ext_feature, own_position, own_feature, neighbor_ids, counts_dev, params_two)
        energies, pullback = jax.vjp(energy_fn, ext_pos, ext_feat, own_pos, features[device])
        grad_ext_pos, grad_ext_feat, grad_own_pos, grad_own_feat = pullback(jnp.ones_like(energies))
        feat_acc = grid_add(feat_acc, index_x, index_y, index_z, grad_ext_feat.reshape(4, 4, 4, G, 4 * channels))
        feat_acc = feat_acc.at[index_x, index_y, index_z].add(grad_own_feat.reshape(2, 2, 2, G, 4 * channels))
        pos_acc = grid_add(pos_acc, index_x, index_y, index_z, grad_ext_pos.T.reshape(4, 4, 4, G, 3))
        pos_acc = pos_acc.at[index_x, index_y, index_z].add(grad_own_pos.T.reshape(2, 2, 2, G, 3))
        return ((feat_acc, pos_acc), energies)
    start = (jnp.zeros(grid_shape + (4 * channels,), jnp.float32), jnp.zeros(grid_shape + (3,), jnp.float32))
    (feat_acc, pos_acc), energies = lax.scan(second, start, device_ids)

    def third_pass(pos_acc, device):
        index_x, index_y, index_z, ext_pos, ext_node, own_pos = device_inputs(device)
        own_node = rows_of(node_all, device)
        neighbor_ids = rows_of(neighbors, device)
        counts_dev = rows_of(neighbor_counts, device)

        def first_map(ext_position, own_position):
            return over_blocks(layer_one_block, ext_position, ext_node, own_position, own_node, neighbor_ids, counts_dev, params_one)
        unused, first_pull = jax.vjp(first_map, ext_pos, own_pos)
        grad_ext_first, grad_own_first = first_pull(feat_acc[index_x, index_y, index_z].reshape(atoms_dev, 4 * channels))
        pos_acc = grid_add(pos_acc, index_x, index_y, index_z, grad_ext_first.T.reshape(4, 4, 4, G, 3))
        pos_acc = pos_acc.at[index_x, index_y, index_z].add(grad_own_first.T.reshape(2, 2, 2, G, 3))
        return (pos_acc, None)
    pos_acc, unused = lax.scan(third_pass, pos_acc, device_ids)
    forces = -pos_acc.reshape(ATOMS, 3).T
    return (energies.reshape(ATOMS), forces)
```

```python
import jax
import jax.numpy as jnp
from jax import lax
from jax.experimental import pallas as pl
from jax.experimental.pallas import tpu as pltpu
from jax.sharding import PartitionSpec as P

F32 = jnp.float32
BF16 = jnp.bfloat16
I32 = jnp.int32
TILE = 256
MAX_TILES = 128
MAX_CORE_TILES = 32
WINDOW = 64
INTERPRET = False

COLUMNS = [(2, 2), (2, 3), (3, 2), (3, 3)] + [
    (y, z) for y in range(1, 5) for z in range(1, 5) if not (y in (2, 3) and z in (2, 3))
]
LIST_BASE = {1: 0, 2: 6, 3: 8, 4: 16}
LIST_STEP = {1: 3, 2: 5, 3: 5, 4: 3}
COORD_BASE = {-1: 2, 0: 10, 1: 18}
COORD_STEP = {-1: 3, 0: 5, 1: 3}


def split(x):
    high = x.astype(BF16)
    return high, (x - high.astype(F32)).astype(BF16)


def three(x, axis):
    high, low = split(x)
    return jnp.concatenate([high, low, high], axis=axis)


def three_weights(w, axis):
    high, low = split(w)
    return jnp.concatenate([high, high, low], axis=axis)


def dot(a, b):
    return lax.dot_general(a, b, (((1,), (0,)), ((), ())), preferred_element_type=F32)


def dot_t(a, b):
    return lax.dot_general(a, b, (((1,), (1,)), ((), ())), preferred_element_type=F32)


def lanes_of(table, index):
    return jnp.take_along_axis(table, index, axis=1, mode="promise_in_bounds")


def silu_pair(x):
    gate = 1.0 / (1.0 + jnp.exp(-x))
    value = x * gate
    return value, gate + value * (1.0 - gate)


def pack_kernel(pos_ref, species_ref, counts_ref, neighbors_ref, out_ref):
    ids = neighbors_ref[...].astype(F32)
    joined = jnp.concatenate([ids[:32], ids[32:]], axis=1)
    for part in range(4):
        out_ref[part] = joined[part * 8 : part * 8 + 8]
    rows = jnp.concatenate(
        [
            pos_ref[...],
            species_ref[...].astype(F32),
            counts_ref[...].astype(F32),
            jnp.zeros((3, 64), F32),
        ],
        axis=0,
    )
    out_ref[4] = jnp.concatenate([rows, rows], axis=1)


def iota(shape, axis):
    return lax.broadcasted_iota(I32, shape, axis)


def main_kernel(
    own_ref,
    low_ref,
    high_ref,
    emb_ref,
    fi_ref,
    fo_ref,
    fs_ref,
    fv_ref,
    fq_ref,
    si_ref,
    so_ref,
    sm_ref,
    rf_ref,
    rs_ref,
    energy_ref,
    up_ref,
    mid_ref,
    down_ref,
    table,
    mask_buf,
    raw,
    rowbuf,
    buf,
    bes_buf,
    dbes_buf,
    pair_buf,
    offs_vmem,
    offs,
    last_row,
    sem,
    acc,
    vec_t,
    slope_t,
    feat_t,
    feat_grad,
    w_acc,
    grad_lhs,
    expand,
    saved_rg,
    saved_slope,
    saved_feat,
    saved_pair_grad,
    box_acc,
    emb_pad,
):
    lane8 = iota((8, 128), 1)
    sub8 = iota((8, 128), 0)
    upper = lane8 >= 64
    layer_refs = {-1: low_ref, 0: own_ref, 1: high_ref}

    for dy in (-1, 0, 1):
        for dz in (-1, 0, 1):
            ref = layer_refs[dz]
            base = COORD_BASE[dy]
            joined = jnp.where(upper, ref[base + COORD_STEP[dy]], ref[base])
            shift_x = jnp.where(upper, 12.0, 0.0)
            shift = jnp.where(
                sub8 == 0, shift_x, jnp.where(sub8 == 1, 12.0 * dy, jnp.where(sub8 == 2, 12.0 * dz, 0.0))
            )
            joined = joined + shift
            row = (dy + 1) * 3 + dz + 1
            for comp in range(5):
                table[comp, row] = jnp.broadcast_to(joined[comp : comp + 1], (8, 128))

    for col, (y, z) in enumerate(COLUMNS):
        dy, b = {1: (-1, 1), 2: (0, 0), 3: (0, 1), 4: (1, 0)}[y]
        dz, c = {1: (-1, 1), 2: (0, 0), 3: (0, 1), 4: (1, 0)}[z]
        y_low = -1 if y <= 2 else 0
        z_low = -1 if z <= 2 else 0
        row_l = (dy + 1) * 3 + dz + 1
        for xd in range(2):
            tile = layer_refs[dz][LIST_BASE[y] + xd * LIST_STEP[y] + c].astype(I32)
            g = tile & 7
            r1 = ((tile >> 3) & 3) + 1
            q1 = ((tile >> 5) & 3) + 1
            p1 = ((tile >> 7) & 3) + 1
            x_side = (1 - ((p1 >> 1) & 1)) ^ xd
            y_index = (q1 >> 1) + (dy - 1 - y_low)
            z_index = (r1 >> 1) + (dz - 1 - z_low)
            lane = x_side * 64 + (p1 & 1) * 32 + (q1 & 1) * 16 + (r1 & 1) * 8 + g
            lane_l = jnp.where(upper, 32, 0) + sub8 + (xd * 64 + b * 16 + c * 8)
            row0 = (y_low + 1) * 3 + z_low + 1
            y_zero = y_index == 0
            z_zero = z_index == 0

            def fetch(comp):
                low = jnp.where(
                    z_zero, lanes_of(table[comp, row0], lane), lanes_of(table[comp, row0 + 1], lane)
                )
                top = jnp.where(
                    z_zero, lanes_of(table[comp, row0 + 3], lane), lanes_of(table[comp, row0 + 4], lane)
                )
                return jnp.where(y_zero, low, top)

            d = [fetch(comp) - lanes_of(table[comp, row_l], lane_l) for comp in range(3)]
            d[0] = jnp.where(d[0] > 12.0, d[0] - 24.0, jnp.where(d[0] < -12.0, d[0] + 24.0, d[0]))
            species = fetch(3)
            count = lanes_of(table[4, row_l], lane_l)
            square = d[0] * d[0] + d[1] * d[1] + d[2] * d[2] + 0.25
            slot = (lane8 & 63).astype(F32)
            reach = (square < 36.0) & (slot < count)
            inside = ((y_index >> 1) == 0) & ((z_index >> 1) == 0)
            live = jnp.where(reach & inside, 1.0, 0.0)
            code = (row0 + y_index * 3 + z_index) * 128 + lane
            at = (col * 2 + xd) * 8
            mask_buf[at : at + 8, :] = live
            raw[0, at : at + 8, :] = d[0]
            raw[1, at : at + 8, :] = d[1]
            raw[2, at : at + 8, :] = d[2]
            raw[3, at : at + 8, :] = species
            raw[4, at : at + 8, :] = code.astype(F32)

    mask = mask_buf[...].astype(BF16)
    upto = jnp.where(iota((128, 128), 0) <= iota((128, 128), 1), 1.0, 0.0).astype(BF16)
    within = dot(mask, upto)
    totals = dot_t(jnp.ones((8, 128), BF16), mask)
    before = jnp.where(iota((256, 256), 0) < iota((256, 256), 1), 1.0, 0.0).astype(BF16)
    starts = dot(totals.astype(BF16), before)
    offs_vmem[:, 0:256] = starts.astype(I32)
    offs_vmem[:, 256:512] = totals.astype(I32)
    copy = pltpu.make_async_copy(offs_vmem, offs, sem)
    copy.start()

    for col, (y, z) in enumerate(COLUMNS):
        dy, b = {1: (-1, 1), 2: (0, 0), 3: (0, 1), 4: (1, 0)}[y]
        dz, c = {1: (-1, 1), 2: (0, 0), 3: (0, 1), 4: (1, 0)}[z]
        row_l = (dy + 1) * 3 + dz + 1
        for xd in range(2):
            at = (col * 2 + xd) * 8
            counted = within[at : at + 8, :]
            wanted = (lane8 + 1).astype(F32)
            place = jnp.zeros((8, 128), I32)
            for step in (64, 32, 16, 8, 4, 2, 1):
                probe = lanes_of(counted, place + (step - 1))
                place = jnp.where(probe < wanted, place + step, place)
            half = jnp.where(place >= 64, 1, 0)
            atom = (at + sub8) * 2 + half
            code_l = row_l * 128 + xd * 64 + b * 16 + c * 8 + sub8 + half * 32
            fields = [lanes_of(raw[k, at : at + 8, :], place) for k in range(5)]
            fields += [atom.astype(F32), code_l.astype(F32)]
            for k, field in enumerate(fields):
                rowbuf[pl.ds(at * 8 + k, 8, stride=8), :] = field

    copy.wait()

    def join_row(r, current):
        start = offs[0, r]
        length = offs[0, 256 + r]
        shift = start & 127
        rolled = pltpu.roll(rowbuf[pl.ds(r * 8, 8), :], shift, 1)
        current = jnp.where(lane8 >= shift, rolled, current)
        buf[pl.ds((start >> 7) * 8, 8), :] = current
        last_row[start >> 8] = r
        return jnp.where(shift + length >= 128, rolled, current)

    current = lax.fori_loop(0, 256, join_row, jnp.zeros((8, 128), F32), unroll=8)
    total = offs[0, 255] + offs[0, 511]
    core_total = offs[0, 64]
    buf[pl.ds((total >> 7) * 8, 8), :] = current
    last_row[jnp.maximum(total - 1, 0) >> 8] = 255
    tiles = (total + (TILE - 1)) // TILE
    core_tiles = (core_total + (TILE - 1)) // TILE

    column_of = jnp.zeros((8, 128), I32)
    for col, (y, z) in enumerate(COLUMNS):
        column_of = jnp.where(lane8 == (y - 1) * 4 + z - 1, col, column_of)

    def basis(chunk, carry):
        at = chunk * 64
        field = [buf[pl.ds(at + k, 8, stride=8), :] for k in range(7)]
        valid = (chunk * 1024 + sub8 * 128 + lane8) < total
        d = [jnp.where(valid, field[k], 100.0) for k in range(3)]
        species = jnp.where(valid, field[3], 0.0)
        code = jnp.where(valid, field[4], 0.0).astype(I32)
        atom = jnp.where(valid, field[5], -1.0)
        code_l = jnp.where(valid, field[6], 0.0)
        square = d[0] * d[0] + d[1] * d[1] + d[2] * d[2] + 0.25
        rho = jnp.sqrt(square)
        inv = 1.0 / rho
        t = jnp.where(rho < 6.0, rho * (1.0 / 6.0), 1.0)
        inside = valid & (rho < 6.0)
        angle = t * 3.14159265358979 - 1.5707963267948966
        a2 = angle * angle
        sin_a = angle * (
            1.0
            + a2
            * (
                -1.0 / 6
                + a2
                * (
                    1.0 / 120
                    + a2 * (-1.0 / 5040 + a2 * (1.0 / 362880 + a2 * (-1.0 / 39916800 + a2 / 6227020800.0)))
                )
            )
        )
        cos_a = 1.0 + a2 * (
            -0.5
            + a2
            * (
                1.0 / 24
                + a2
                * (
                    -1.0 / 720
                    + a2
                    * (1.0 / 40320 + a2 * (-1.0 / 3628800 + a2 * (1.0 / 479001600 - a2 / 87178291200.0)))
                )
            )
        )
        sine, cosine = cos_a, -sin_a
        t2 = t * t
        t5 = t2 * t2 * t
        f = 1.0 + t5 * t * (-28.0 + t * (48.0 - 21.0 * t))
        f = jnp.where(inside, f, 0.0)
        one = 1.0 - t
        df = jnp.where(inside, -28.0 * t5 * one * one, 0.0)
        scale = 0.5773502691896258
        amount = scale * inv * f
        slope = scale * inv * (df - inv * f)
        s_prev, c_prev = jnp.zeros((8, 128), F32), jnp.ones((8, 128), F32)
        s_now, c_now = sine, cosine
        for n in range(8):
            bes_buf[pl.ds(at + n, 8, stride=8), :] = s_now * amount
            dbes_buf[pl.ds(at + n, 8, stride=8), :] = (
                c_now * amount * ((n + 1) * 0.5235987755982988) + s_now * slope
            )
            s_now, s_prev = 2.0 * cosine * s_now - s_prev, s_now
            c_now, c_prev = 2.0 * cosine * c_now - c_prev, c_now
        row = code >> 7
        lane = code & 127
        row_y = jnp.where(row >= 6, 2, jnp.where(row >= 3, 1, 0))
        row_z = row - 3 * row_y
        y = row_y * 2 + ((lane >> 4) & 1) - 1
        z = row_z * 2 + ((lane >> 3) & 1) - 1
        near = (y >= 0) & (y < 4) & (z >= 0) & (z < 4)
        column = lanes_of(column_of, jnp.where(near, y * 4 + z, 0))
        source = column * 32 + ((lane >> 6) & 1) * 16 + (lane & 7) * 2 + ((lane >> 5) & 1)
        source = jnp.where(near, source, -1)
        both = code.astype(F32) * 2048.0 + code_l
        kept = [d[0] * inv, d[1] * inv, d[2] * inv, inv, species, source.astype(F32), atom, both]
        for k, value in enumerate(kept):
            pair_buf[pl.ds(at + k, 8, stride=8), :] = value
        return carry

    lax.fori_loop(0, (total + 1023) // 1024, basis, 0)

    fi3 = jnp.concatenate([fi_ref[...], jnp.zeros((24, 64), F32)], axis=0)
    si3 = jnp.concatenate([si_ref[...], jnp.zeros((24, 64), F32)], axis=0)

    def inner_weights(padded):
        w = padded.T[:, 0:8]
        high = w.astype(BF16).astype(F32)
        low = w - high
        return jnp.concatenate([high, high, low, jnp.zeros((64, 8), F32)], axis=1).astype(BF16)

    def inner_back(ref):
        w = jnp.concatenate([ref[...], jnp.zeros((8, 64), F32)], axis=0)
        return three_weights(w, 1)

    fi_t3 = inner_weights(fi3)
    si_t3 = inner_weights(si3)
    fi_b3 = inner_back(fi_ref)
    si_b3 = inner_back(si_ref)
    fo_t3 = three_weights(fo_ref[...].T, 1)
    so_t3 = three_weights(so_ref[...].T, 1)
    fo_b3 = three_weights(fo_ref[...], 1)
    so_b3 = three_weights(so_ref[...], 1)
    emb_pad[...] = jnp.zeros((128, 128), F32)
    emb_pad[0:89, :] = emb_ref[...]
    emb_t2 = jnp.concatenate(split(emb_pad[...].T), axis=1)

    def tile_rows(ref, t):
        at = t * 16
        return jnp.concatenate([ref[pl.ds(at, 8), :], ref[pl.ds(at + 8, 8), :]], axis=1)

    def hidden_of(t, weights):
        bes = tile_rows(bes_buf, t)
        high = bes.astype(BF16).astype(F32)
        stack = jnp.concatenate([high, bes - high, high, jnp.zeros((8, TILE), F32)], axis=0)
        return silu_pair(dot(weights, stack.astype(BF16)))

    def onehot(index_row, rows):
        hit = iota((rows, index_row.shape[1]), 0) == index_row.astype(I32)
        return jnp.where(hit, 1.0, 0.0).astype(BF16)

    def sender_of(species_row):
        hot = onehot(species_row, 128)
        return dot(emb_t2, jnp.concatenate([hot, hot], axis=0))

    def first_of(t):
        return jnp.where(t == 0, 0, last_row[jnp.maximum(t - 1, 0)]) * 2

    acc[...] = jnp.zeros(acc.shape, F32)

    def layer_one(t, carry):
        hidden, slope = hidden_of(t, fi_t3)
        saved_slope[t] = slope
        weights = dot(fo_t3, three(hidden, 0))
        pair = tile_rows(pair_buf, t)
        sender = sender_of(pair[4:5])
        m_high, m_low = split(weights[0:128] * sender)
        rg = weights[128:256] * sender
        saved_rg[t] = rg
        v_high, v_low = split(rg)
        saved_pair_grad[t] = jnp.zeros((8, TILE), F32)
        unit = [split(pair[k : k + 1]) for k in range(3)]
        base = first_of(t) & -8
        windows = (last_row[t] * 2 + 1 - base) // WINDOW + 1

        def window(w, carry):
            at = base + w * WINDOW
            hot = onehot(pair[6:7] - at.astype(F32), WINDOW)
            u_high = jnp.concatenate([hot * high for high, _ in unit], axis=0)
            u_low = jnp.concatenate([hot * low for _, low in unit], axis=0)
            m = dot_t(hot, m_high) + dot_t(hot, m_low)
            v = dot_t(u_high, v_high) + dot_t(u_high, v_low) + dot_t(u_low, v_high)
            rows = pl.ds(pl.multiple_of(at, 8), WINDOW)
            acc[0, rows, :] += m
            for x in range(3):
                acc[1 + x, rows, :] += v[x * WINDOW : (x + 1) * WINDOW]
            return carry

        return lax.fori_loop(0, windows, window, carry)

    lax.fori_loop(0, tiles, layer_one, 0)

    parts = []
    for group in range(4):
        merged = None
        for sub in range(4):
            col = group * 4 + sub
            y, z = COLUMNS[col]
            dy, b = {1: (-1, 1), 2: (0, 0), 3: (0, 1), 4: (1, 0)}[y]
            dz, c = {1: (-1, 1), 2: (0, 0), 3: (0, 1), 4: (1, 0)}[z]
            local = lane8 & 31
            index = ((local >> 4) & 1) * 64 + (local & 1) * 32 + ((local >> 1) & 7) + b * 16 + c * 8
            got = lanes_of(table[3, (dy + 1) * 3 + dz + 1], index)
            merged = got if merged is None else jnp.where((lane8 >> 5) == sub, got, merged)
        parts.append(merged)
    species_row = jnp.concatenate(parts, axis=1)[0:1]
    node_t = sender_of(species_row)
    fv_t3 = three_weights(fv_ref[...].T, 1)
    square_t = jnp.zeros((128, 512), F32)
    for x in range(3):
        v3 = three(acc[1 + x, 0:512, :] * 0.25, 1)
        value = dot_t(fv_t3, v3)
        vec_t[x] = value
        square_t = square_t + value * value
        high, low = split(value)
        feat_t[0, 128 + x * 128 : 256 + x * 128, :] = high
        feat_t[1, 128 + x * 128 : 256 + x * 128, :] = low
    fs_t3 = three_weights(fs_ref[...].T, 1)
    fq_t3 = three_weights(fq_ref[...].T, 1)
    pre = dot_t(fs_t3, three(acc[0, 0:512, :] * 0.25, 1))
    pre = pre + dot(fs_t3, three(node_t, 0)) + dot(fq_t3, three(square_t, 0))
    scal_t, slope = silu_pair(pre)
    slope_t[...] = slope
    high, low = split(scal_t)
    feat_t[0, 0:128, :] = high
    feat_t[1, 0:128, :] = low
    scal_core = scal_t[:, 0:128]

    w_acc[...] = jnp.zeros((128, 128), F32)

    def layer_two(t, carry):
        hidden, _ = hidden_of(t, si_t3)
        weights = dot(so_t3, three(hidden, 0))
        pair = tile_rows(pair_buf, t)
        hot = onehot(pair[5:6], 512)
        feat = dot(feat_t[0], hot) + dot(feat_t[1], hot)
        saved_feat[t] = feat
        proj = pair[0:1] * feat[128:256] + pair[1:2] * feat[256:384] + pair[2:3] * feat[384:512]
        high, low = split(weights[0:128] * feat[0:128] + weights[128:256] * proj)
        member = onehot(pair[6:7], 128)
        w_acc[...] += dot_t(high, member) + dot_t(low, member)
        return carry

    lax.fori_loop(0, core_tiles, layer_two, 0)

    mixed = w_acc[...] * 0.25 + scal_core
    rs_col = jnp.broadcast_to(rs_ref[...], (128, 128)).T
    rf_col = jnp.broadcast_to(rf_ref[...], (128, 128)).T
    out, out_slope = silu_pair(dot(three_weights(sm_ref[...].T, 1), three(mixed, 0)))
    energy = jnp.sum(out * rs_col + scal_core * rf_col, axis=0, keepdims=True)
    index = (((lane8 >> 3) & 3) * 16 + (lane8 & 7)) * 2 + ((lane8 >> 5) & 1)
    index = jnp.where(lane8 < 64, ((lane8 >> 3) & 3) * 32 + (lane8 & 7) * 2 + ((lane8 >> 5) & 1), 0)
    energy_ref[...] = lanes_of(jnp.broadcast_to(energy, (8, 128)), index)[0:1, 0:64]

    mixed_grad = dot(three_weights(sm_ref[...], 1), three(rs_col * out_slope, 0))
    w_grad2 = jnp.concatenate(split(mixed_grad * 0.25), axis=1)
    feat_grad[...] = jnp.zeros((512, 512), F32)
    feat_grad[0:128, 0:128] = mixed_grad + rf_col

    def radial_back(t, slope, grad, outer3, inner3):
        hidden_grad = dot(outer3, three(grad, 0)) * slope
        bes_grad = dot(inner3, three(hidden_grad, 0))[0:8]
        return jnp.sum(bes_grad * tile_rows(dbes_buf, t), axis=0, keepdims=True)

    def layer_two_back(t, carry):
        hidden, slope = hidden_of(t, si_t3)
        weights = dot(so_t3, three(hidden, 0))
        pair = tile_rows(pair_buf, t)
        feat = saved_feat[t]
        member = onehot(pair[6:7], 128)
        w_grad = dot(w_grad2, jnp.concatenate([member, member], axis=0))
        proj = pair[0:1] * feat[128:256] + pair[1:2] * feat[256:384] + pair[2:3] * feat[384:512]
        radial_grad = jnp.concatenate([w_grad * feat[0:128], w_grad * proj], axis=0)
        rho_grad = radial_back(t, slope, radial_grad, so_b3, si_b3)
        proj_grad = w_grad * weights[128:256]
        grads = [rho_grad]
        sends = [w_grad * weights[0:128]]
        for x in range(3):
            part = feat[128 + x * 128 : 256 + x * 128]
            grads.append(jnp.sum(proj_grad * part, axis=0, keepdims=True))
            sends.append(proj_grad * pair[x : x + 1])
        saved_pair_grad[t] = jnp.concatenate(grads + [jnp.zeros((4, TILE), F32)], axis=0)
        high, low = split(jnp.concatenate(sends, axis=0))
        hot = onehot(pair[5:6], 512)
        feat_grad[...] += dot_t(high, hot) + dot_t(low, hot)
        return carry

    lax.fori_loop(0, core_tiles, layer_two_back, 0)

    pre_grad3 = three(feat_grad[0:128, :] * slope_t[...], 0)
    m_grad = dot(three_weights(fs_ref[...], 1), pre_grad3)
    square_grad = dot(three_weights(fq_ref[...], 1), pre_grad3)
    fv_b3 = three_weights(fv_ref[...], 1)
    message_grads = [m_grad]
    for x in range(3):
        part = feat_grad[128 + x * 128 : 256 + x * 128, :] + 2.0 * vec_t[x] * square_grad
        message_grads.append(dot(fv_b3, three(part, 0)))
    for kind in range(4):
        high, low = split(message_grads[kind] * 0.25)
        for w in range(4):
            grad_lhs[w, kind * 128 : (kind + 1) * 128, 0:128] = high[:, w * 128 : (w + 1) * 128]
            grad_lhs[w, kind * 128 : (kind + 1) * 128, 128:256] = low[:, w * 128 : (w + 1) * 128]

    box_acc[...] = jnp.zeros((96, 128), F32)

    def layer_one_back(t, carry):
        pair = tile_rows(pair_buf, t)
        first = first_of(t) >> 7
        last = (last_row[t] * 2 + 1) >> 7

        def expanded(w):
            member = onehot(pair[6:7] - (w * 128).astype(F32), 128)
            return dot(grad_lhs[w], jnp.concatenate([member, member], axis=0))

        expand[...] = expanded(first)

        def more(w, carry):
            expand[...] += expanded(w)
            return carry

        lax.fori_loop(first + 1, last + 1, more, 0)
        sender = sender_of(pair[4:5])
        rg = saved_rg[t]
        v_grad = [expand[128 + x * 128 : 256 + x * 128, :] for x in range(3)]
        along = pair[0:1] * v_grad[0] + pair[1:2] * v_grad[1] + pair[2:3] * v_grad[2]
        radial_grad = jnp.concatenate([expand[0:128, :] * sender, along * sender], axis=0)
        earlier = saved_pair_grad[t]
        rho_grad = radial_back(t, saved_slope[t], radial_grad, fo_b3, fi_b3) + earlier[0:1]
        unit_grad = [
            jnp.sum(rg * v_grad[x], axis=0, keepdims=True) + earlier[1 + x : 2 + x] for x in range(3)
        ]
        unit = [pair[x : x + 1] for x in range(3)]
        inner = unit[0] * unit_grad[0] + unit[1] * unit_grad[1] + unit[2] * unit_grad[2]
        inv = pair[3:4]
        values = []
        for x in range(3):
            value = (unit_grad[x] - unit[x] * inner) * inv + rho_grad * unit[x]
            high = value.astype(BF16).astype(F32)
            values += [high, value - high]
        both = pair[7:8].astype(I32)

        def spread(code, sign):
            row = jnp.broadcast_to(code >> 7, (16, TILE)) == iota((16, TILE), 0)
            stack = [jnp.where(row, sign * value, 0.0) for value in values]
            lane = jnp.where(iota((128, TILE), 0) == (code & 127), 1.0, 0.0).astype(BF16)
            return dot_t(jnp.concatenate(stack, axis=0).astype(BF16), lane)

        box_acc[...] += spread(both >> 11, 1.0) + spread(both & 2047, -1.0)
        return carry

    lax.fori_loop(0, tiles, layer_one_back, 0)

    for comp in range(3):
        grid = box_acc[comp * 32 : comp * 32 + 16, :] + box_acc[comp * 32 + 16 : comp * 32 + 32, :]
        for dz, ref in ((-1, down_ref), (0, mid_ref), (1, up_ref)):
            for dy in range(3):
                row = dy * 3 + dz + 1
                ref[dy, comp : comp + 1, :] = grid[row : row + 1, :]
    for ref in (down_ref, mid_ref, up_ref):
        for dy in range(3):
            ref[dy, 3:8, :] = jnp.zeros((5, 128), F32)


def pair_program(own, low, high, weights):
    vm = pltpu.VMEM
    pair_rows = (MAX_TILES * 2 + 8) * 8
    scratch = [
        vm((5, 9, 8, 128), F32),
        vm((256, 128), F32),
        vm((5, 256, 128), F32),
        vm((2048, 128), F32),
        vm((pair_rows, 128), F32),
        vm((pair_rows, 128), F32),
        vm((pair_rows, 128), F32),
        vm((pair_rows, 128), F32),
        vm((8, 512), I32),
        pltpu.SMEM((8, 512), I32),
        pltpu.SMEM((256,), I32),
        pltpu.SemaphoreType.DMA,
        vm((4, 512 + WINDOW, 128), F32),
        vm((3, 128, 512), F32),
        vm((128, 512), F32),
        vm((2, 512, 512), BF16),
        vm((512, 512), F32),
        vm((128, 128), F32),
        vm((4, 512, 256), BF16),
        vm((512, TILE), F32),
        vm((MAX_TILES, 128, TILE), F32),
        vm((MAX_TILES, 64, TILE), F32),
        vm((MAX_CORE_TILES, 512, TILE), F32),
        vm((MAX_TILES, 8, TILE), F32),
        vm((96, 128), F32),
        vm((128, 128), F32),
    ]
    whole = pl.BlockSpec(memory_space=pltpu.VMEM)
    piece = jax.ShapeDtypeStruct((3, 8, 128), F32)
    return pl.pallas_call(
        main_kernel,
        out_shape=(jax.ShapeDtypeStruct((1, 64), F32), piece, piece, piece),
        in_specs=[whole] * (3 + len(weights)),
        out_specs=(whole,) * 4,
        scratch_shapes=scratch,
        compiler_params=pltpu.CompilerParams(vmem_limit_bytes=60 * 1024 * 1024),
        interpret=INTERPRET,
    )(own, low, high, *weights)


def pack(positions, species, counts, neighbors):
    whole = pl.BlockSpec(memory_space=pltpu.VMEM)
    return pl.pallas_call(
        pack_kernel,
        out_shape=jax.ShapeDtypeStruct((5, 8, 128), F32),
        in_specs=[whole] * 4,
        out_specs=whole,
        interpret=INTERPRET,
    )(positions, species.reshape(1, 64), counts.reshape(1, 64), neighbors)


def join_y(own, below, above):
    return jnp.concatenate(
        [below[2:5], below[7:10], own, above[0:2], above[4:7], above[9:10]], axis=0
    )


def ring(axis, step):
    count = lax.axis_size(axis)
    return [(i, (i + step) % count) for i in range(count)]


def shards(
    positions,
    species,
    neighbors,
    neighbor_counts,
    embedding,
    first_inner,
    first_outer,
    first_scalar,
    first_vector,
    first_square,
    second_inner,
    second_outer,
    second_mix,
    readout_first,
    readout_second,
):
    packed = pack(positions, species, neighbor_counts, neighbors)
    partner = lax.ppermute(packed, "gx", ring("gx", 1))
    both = jnp.concatenate([packed, partner], axis=0)
    below = lax.ppermute(both, "gy", ring("gy", 1))
    above = lax.ppermute(both, "gy", ring("gy", -1))
    layer = join_y(both, below, above)
    low = lax.ppermute(layer, "gz", ring("gz", 1))
    high = lax.ppermute(layer, "gz", ring("gz", -1))
    weights = (
        embedding,
        first_inner,
        first_outer,
        first_scalar,
        first_vector,
        first_square,
        second_inner,
        second_outer,
        second_mix,
        readout_first.reshape(1, 128),
        readout_second.reshape(1, 128),
    )
    energy, up, mid, down = pair_program(layer, low, high, weights)
    folded = mid + lax.ppermute(up, "gz", ring("gz", 1)) + lax.ppermute(down, "gz", ring("gz", -1))
    total = folded[1] + lax.ppermute(folded[2], "gy", ring("gy", 1))
    total = total + lax.ppermute(folded[0], "gy", ring("gy", -1))
    return (energy.reshape(64), -total[0:3, 0:64])


def solution(mesh):
    spread = ("gx", "gy", "gz")
    placed = (P(None, spread), P(spread), P(spread, None), P(spread)) + (P(),) * 11
    return jax.shard_map(
        shards,
        mesh=mesh,
        in_specs=placed,
        out_specs=(P(spread), P(None, spread)),
        check_vma=False,
    )
```

```python
import jax
import jax.numpy as jnp
from jax import lax
from jax.experimental import pallas as pl
from jax.experimental.pallas import tpu as pltpu
from jax.sharding import PartitionSpec as P

F32 = jnp.float32
BF16 = jnp.bfloat16
I32 = jnp.int32
TILE = 256
MAX_TILES = 129
MAX_CORE_TILES = 32
WINDOW = 64
UNROLL = 3
INTERPRET = False

COLUMNS = [
    (1 + ((col >> 3) * 2 + ((col >> 1) & 1) + 1) % 4, 1 + (((col >> 2) & 1) * 2 + (col & 1) + 1) % 4)
    for col in range(16)
]
LIST_BASE = {1: 0, 2: 6, 3: 8, 4: 16}
LIST_STEP = {1: 3, 2: 5, 3: 5, 4: 3}
COORD_BASE = {-1: 2, 0: 10, 1: 18}
COORD_STEP = {-1: 3, 0: 5, 1: 3}


def split(x):
    high = x.astype(BF16)
    return high, (x - high.astype(F32)).astype(BF16)


def three(x, axis):
    high, low = split(x)
    return jnp.concatenate([high, low, high], axis=axis)


def three_weights(w, axis):
    high, low = split(w)
    return jnp.concatenate([high, high, low], axis=axis)


def dot(a, b):
    return lax.dot_general(a, b, (((1,), (0,)), ((), ())), preferred_element_type=F32)


def dot_t(a, b):
    return lax.dot_general(a, b, (((1,), (1,)), ((), ())), preferred_element_type=F32)


def lanes_of(table, index):
    return jnp.take_along_axis(table, index, axis=1, mode="promise_in_bounds")


def silu_pair(x):
    gate = 1.0 / (1.0 + jnp.exp(-x))
    value = x * gate
    return value, gate + value * (1.0 - gate)


def pack_kernel(pos_ref, species_ref, counts_ref, neighbors_ref, out_ref):
    ids = neighbors_ref[...].astype(F32)
    joined = jnp.concatenate([ids[:32], ids[32:]], axis=1)
    for part in range(4):
        out_ref[part] = joined[part * 8 : part * 8 + 8]
    rows = jnp.concatenate(
        [
            pos_ref[...],
            species_ref[...].astype(F32),
            counts_ref[...].astype(F32),
            jnp.zeros((3, 64), F32),
        ],
        axis=0,
    )
    out_ref[4] = jnp.concatenate([rows, rows], axis=1)


def iota(shape, axis):
    return lax.broadcasted_iota(I32, shape, axis)


def main_kernel(
    own_ref,
    low_ref,
    high_ref,
    emb_ref,
    fi_ref,
    fo_ref,
    fs_ref,
    fv_ref,
    fq_ref,
    si_ref,
    so_ref,
    sm_ref,
    rf_ref,
    rs_ref,
    energy_ref,
    up_ref,
    mid_ref,
    down_ref,
    table,
    mask_buf,
    lists,
    raw,
    counted_buf,
    rowbuf,
    buf,
    bes_buf,
    dbes_buf,
    pair_buf,
    offs_vmem,
    offs,
    last_row,
    sem,
    acc,
    vec_t,
    slope_t,
    feat_t,
    feat_grad,
    w_acc,
    grad_lhs,
    expand,
    saved_rg,
    saved_slope,
    saved_feat,
    saved_pair_grad,
    box_acc,
    emb_pad,
):
    lane8 = iota((8, 128), 1)
    sub8 = iota((8, 128), 0)
    upper = lane8 >= 64
    layer_refs = {-1: low_ref, 0: own_ref, 1: high_ref}

    for dy in (-1, 0, 1):
        for dz in (-1, 0, 1):
            ref = layer_refs[dz]
            base = COORD_BASE[dy]
            joined = jnp.where(upper, ref[base + COORD_STEP[dy]], ref[base])
            shift_x = jnp.where(upper, 12.0, 0.0)
            shift = jnp.where(
                sub8 == 0, shift_x, jnp.where(sub8 == 1, 12.0 * dy, jnp.where(sub8 == 2, 12.0 * dz, 0.0))
            )
            joined = joined + shift
            row = (dy + 1) * 3 + dz + 1
            for comp in range(5):
                table[comp, row] = jnp.broadcast_to(joined[comp : comp + 1], (8, 128))

    for col, (y, z) in enumerate(COLUMNS):
        layer = layer_refs[(z >> 1) - 1]
        for xd in range(2):
            lists[col * 2 + xd] = layer[LIST_BASE[y] + xd * LIST_STEP[y] + (z & 1)]

    def place_of(part):
        col, xd = part >> 1, part & 1
        y = 1 + (((col >> 3) * 2 + ((col >> 1) & 1) + 1) & 3)
        z = 1 + ((((col >> 2) & 1) * 2 + (col & 1) + 1) & 3)
        lane = xd * 64 + (y & 1) * 16 + (z & 1) * 8
        return y, z, xd, (y >> 1) * 3 + (z >> 1), lane

    def distances(part, carry):
        y, z, xd, row_l, base_l = place_of(part)
        y_low = jnp.where(y >= 3, 1, 0)
        z_low = jnp.where(z >= 3, 1, 0)
        row0 = y_low * 3 + z_low
        tile = lists[part].astype(I32)
        r1 = ((tile >> 3) & 3) + 1
        q1 = ((tile >> 5) & 3) + 1
        p1 = ((tile >> 7) & 3) + 1
        x_side = (1 - ((p1 >> 1) & 1)) ^ xd
        y_index = (q1 >> 1) + ((y >> 1) - 1 - y_low)
        z_index = (r1 >> 1) + ((z >> 1) - 1 - z_low)
        lane = x_side * 64 + (p1 & 1) * 32 + (q1 & 1) * 16 + (r1 & 1) * 8 + (tile & 7)
        lane_l = jnp.where(upper, 32, 0) + sub8 + base_l
        y_zero = y_index == 0
        z_zero = z_index == 0

        def fetch(comp):
            low = jnp.where(
                z_zero, lanes_of(table[comp, row0], lane), lanes_of(table[comp, row0 + 1], lane)
            )
            top = jnp.where(
                z_zero, lanes_of(table[comp, row0 + 3], lane), lanes_of(table[comp, row0 + 4], lane)
            )
            return jnp.where(y_zero, low, top)

        d = [fetch(comp) - lanes_of(table[comp, row_l], lane_l) for comp in range(3)]
        d[0] = jnp.where(d[0] > 12.0, d[0] - 24.0, jnp.where(d[0] < -12.0, d[0] + 24.0, d[0]))
        species = fetch(3)
        count = lanes_of(table[4, row_l], lane_l)
        square = d[0] * d[0] + d[1] * d[1] + d[2] * d[2] + 0.25
        slot = (lane8 & 63).astype(F32)
        reach = (square < 36.0) & (slot < count)
        inside = ((y_index >> 1) == 0) & ((z_index >> 1) == 0)
        live = jnp.where(reach & inside, 1.0, 0.0)
        code = (row0 + y_index * 3 + z_index) * 128 + lane
        rows = pl.ds(pl.multiple_of(part * 8, 8), 8)
        mask_buf[rows, :] = live
        raw[0, rows, :] = d[0]
        raw[1, rows, :] = d[1]
        raw[2, rows, :] = d[2]
        raw[3, rows, :] = species
        raw[4, rows, :] = code.astype(F32)
        return carry

    lax.fori_loop(0, 32, distances, 0, unroll=4)

    mask = mask_buf[...].astype(BF16)
    upto = jnp.where(iota((128, 128), 0) <= iota((128, 128), 1), 1.0, 0.0).astype(BF16)
    within = dot(mask, upto)
    totals = dot_t(jnp.ones((8, 128), BF16), mask)
    before = jnp.where(iota((256, 256), 0) < iota((256, 256), 1), 1.0, 0.0).astype(BF16)
    starts = dot(totals.astype(BF16), before)
    offs_vmem[:, 0:256] = starts.astype(I32)
    offs_vmem[:, 256:512] = totals.astype(I32)
    copy = pltpu.make_async_copy(offs_vmem, offs, sem)
    copy.start()

    counted_buf[...] = within

    def to_front(part, carry):
        _, _, _, row_l, base_l = place_of(part)
        at = pl.multiple_of(part * 8, 8)
        rows = pl.ds(at, 8)
        counted = counted_buf[rows, :]
        wanted = (lane8 + 1).astype(F32)
        place = jnp.zeros((8, 128), I32)
        for step in (64, 32, 16, 8, 4, 2, 1):
            probe = lanes_of(counted, place + (step - 1))
            place = jnp.where(probe < wanted, place + step, place)
        half = jnp.where(place >= 64, 1, 0)
        atom = (at + sub8) * 2 + half
        code_l = row_l * 128 + base_l + sub8 + half * 32
        fields = [lanes_of(raw[k, rows, :], place) for k in range(5)]
        fields += [atom.astype(F32), code_l.astype(F32)]
        for k, field in enumerate(fields):
            rowbuf[pl.ds(at * 8 + k, 8, stride=8), :] = field
        return carry

    lax.fori_loop(0, 32, to_front, 0, unroll=16)

    copy.wait()

    def join_row(r, current):
        start = offs[0, r]
        length = offs[0, 256 + r]
        shift = start & 127
        rolled = pltpu.roll(rowbuf[pl.ds(r * 8, 8), :], shift, 1)
        current = jnp.where(lane8 >= shift, rolled, current)
        buf[pl.ds((start >> 7) * 8, 8), :] = current
        last_row[start >> 8] = r
        return jnp.where(shift + length >= 128, rolled, current)

    current = lax.fori_loop(0, 256, join_row, jnp.zeros((8, 128), F32), unroll=16)
    total = offs[0, 255] + offs[0, 511]
    core_total = offs[0, 64]
    buf[pl.ds((total >> 7) * 8, 8), :] = current
    last_row[jnp.maximum(total - 1, 0) >> 8] = 255
    tiles = (total + (TILE - 1)) // TILE
    core_tiles = (core_total + (TILE - 1)) // TILE
    steps = (tiles + UNROLL - 1) // UNROLL

    def basis(chunk, carry):
        at = chunk * 64
        field = [buf[pl.ds(at + k, 8, stride=8), :] for k in range(7)]
        valid = (chunk * 1024 + sub8 * 128 + lane8) < total
        d = [jnp.where(valid, field[k], 100.0) for k in range(3)]
        species = jnp.where(valid, field[3], 0.0)
        code = jnp.where(valid, field[4], 0.0).astype(I32)
        atom = jnp.where(valid, field[5], -1.0)
        code_l = jnp.where(valid, field[6], 0.0)
        square = d[0] * d[0] + d[1] * d[1] + d[2] * d[2] + 0.25
        rho = jnp.sqrt(square)
        inv = 1.0 / rho
        t = jnp.where(rho < 6.0, rho * (1.0 / 6.0), 1.0)
        inside = valid & (rho < 6.0)
        angle = t * 3.14159265358979 - 1.5707963267948966
        a2 = angle * angle
        sin_a = angle * (
            1.0
            + a2
            * (
                -1.0 / 6
                + a2
                * (
                    1.0 / 120
                    + a2 * (-1.0 / 5040 + a2 * (1.0 / 362880 + a2 * (-1.0 / 39916800 + a2 / 6227020800.0)))
                )
            )
        )
        cos_a = 1.0 + a2 * (
            -0.5
            + a2
            * (
                1.0 / 24
                + a2
                * (
                    -1.0 / 720
                    + a2
                    * (1.0 / 40320 + a2 * (-1.0 / 3628800 + a2 * (1.0 / 479001600 - a2 / 87178291200.0)))
                )
            )
        )
        sine, cosine = cos_a, -sin_a
        t2 = t * t
        t5 = t2 * t2 * t
        f = 1.0 + t5 * t * (-28.0 + t * (48.0 - 21.0 * t))
        f = jnp.where(inside, f, 0.0)
        one = 1.0 - t
        df = jnp.where(inside, -28.0 * t5 * one * one, 0.0)
        scale = 0.5773502691896258
        amount = scale * inv * f
        slope = scale * inv * (df - inv * f)
        s_prev, c_prev = jnp.zeros((8, 128), F32), jnp.ones((8, 128), F32)
        s_now, c_now = sine, cosine
        for n in range(8):
            bes_buf[pl.ds(at + n, 8, stride=8), :] = s_now * amount
            dbes_buf[pl.ds(at + n, 8, stride=8), :] = (
                c_now * amount * ((n + 1) * 0.5235987755982988) + s_now * slope
            )
            s_now, s_prev = 2.0 * cosine * s_now - s_prev, s_now
            c_now, c_prev = 2.0 * cosine * c_now - c_prev, c_now
        row = code >> 7
        lane = code & 127
        row_y = jnp.where(row >= 6, 2, jnp.where(row >= 3, 1, 0))
        row_z = row - 3 * row_y
        y = row_y * 2 + ((lane >> 4) & 1) - 1
        z = row_z * 2 + ((lane >> 3) & 1) - 1
        near = (y >= 0) & (y < 4) & (z >= 0) & (z < 4)
        y = (y + 3) & 3
        z = (z + 3) & 3
        column = (y >> 1) * 8 + (z >> 1) * 4 + (y & 1) * 2 + (z & 1)
        source = column * 32 + ((lane >> 6) & 1) * 16 + (lane & 7) * 2 + ((lane >> 5) & 1)
        source = jnp.where(near, source, -1)
        both = code.astype(F32) * 2048.0 + code_l
        kept = [d[0] * inv, d[1] * inv, d[2] * inv, inv, species, source.astype(F32), atom, both]
        for k, value in enumerate(kept):
            pair_buf[pl.ds(at + k, 8, stride=8), :] = value
        return carry

    lax.fori_loop(0, (steps * UNROLL * TILE + 1023) // 1024, basis, 0)

    fi3 = jnp.concatenate([fi_ref[...], jnp.zeros((24, 64), F32)], axis=0)
    si3 = jnp.concatenate([si_ref[...], jnp.zeros((24, 64), F32)], axis=0)

    def inner_weights(padded):
        w = padded.T[:, 0:8]
        high = w.astype(BF16).astype(F32)
        low = w - high
        return jnp.concatenate([high, high, low, jnp.zeros((64, 8), F32)], axis=1).astype(BF16)

    def inner_back(ref):
        w = jnp.concatenate([ref[...], jnp.zeros((8, 64), F32)], axis=0)
        return three_weights(w, 1)

    fi_t3 = inner_weights(fi3)
    si_t3 = inner_weights(si3)
    fi_b3 = inner_back(fi_ref)
    si_b3 = inner_back(si_ref)
    fo_t3 = three_weights(fo_ref[...].T, 1)
    so_t3 = three_weights(so_ref[...].T, 1)
    fo_b3 = jnp.concatenate(split(fo_ref[...]), axis=0)
    so_b3 = jnp.concatenate(split(so_ref[...]), axis=0)
    emb_pad[...] = jnp.zeros((128, 128), F32)
    emb_pad[0:89, :] = emb_ref[...]
    emb_t2 = jnp.concatenate(split(emb_pad[...].T), axis=1)

    def tile_rows(ref, t):
        at = t * 16
        return jnp.concatenate([ref[pl.ds(at, 8), :], ref[pl.ds(at + 8, 8), :]], axis=1)

    def hidden_of(t, weights):
        bes = tile_rows(bes_buf, t)
        high = bes.astype(BF16).astype(F32)
        stack = jnp.concatenate([high, bes - high, high, jnp.zeros((8, TILE), F32)], axis=0)
        return silu_pair(dot(weights, stack.astype(BF16)))

    def onehot(index_row, rows):
        hit = iota((rows, index_row.shape[1]), 0) == index_row.astype(I32)
        return jnp.where(hit, 1.0, 0.0).astype(BF16)

    def sender_of(species_row):
        hot = onehot(species_row, 128)
        return dot(emb_t2, jnp.concatenate([hot, hot], axis=0))

    def first_of(t):
        before = jnp.clip(t - 1, 0, jnp.maximum(tiles - 1, 0))
        return jnp.where(t == 0, 0, last_row[before]) * 2

    acc[...] = jnp.zeros(acc.shape, F32)

    def layer_one(step, carry):
        done = []
        for part in range(UNROLL):
            t = step * UNROLL + part
            hidden, slope = hidden_of(t, fi_t3)
            saved_slope[t] = slope
            weights = dot(fo_t3, three(hidden, 0))
            pair = tile_rows(pair_buf, t)
            sender = sender_of(pair[4:5])
            message = split(weights[0:128] * sender)
            rg = weights[128:256] * sender
            saved_rg[t] = rg
            saved_pair_grad[t] = jnp.zeros((8, TILE), F32)
            done.append((t, first_of(t) & -8, pair, message, split(rg)))

        def window(entry, w):
            _, base, pair, (m_high, m_low), (v_high, v_low) = entry
            at = base + w * WINDOW
            unit = [split(pair[k : k + 1]) for k in range(3)]
            hot = onehot(pair[6:7] - at.astype(F32), WINDOW)
            u_high = jnp.concatenate([hot * high for high, _ in unit], axis=0)
            u_low = jnp.concatenate([hot * low for _, low in unit], axis=0)
            m = dot_t(hot, m_high) + dot_t(hot, m_low)
            v = dot_t(u_high, v_high) + dot_t(u_high, v_low) + dot_t(u_low, v_high)
            return pl.ds(pl.multiple_of(at, 8), WINDOW), m, v

        def add(rows, m, v):
            acc[0, rows, :] += m
            for x in range(3):
                acc[1 + x, rows, :] += v[x * WINDOW : (x + 1) * WINDOW]

        for sums in [window(entry, 0) for entry in done]:
            add(*sums)
        counts = [
            jnp.where(t < tiles, (last_row[t] * 2 + 1 - base) // WINDOW + 1, 1)
            for t, base, _, _, _ in done
        ]
        most = counts[0]
        for count in counts[1:]:
            most = jnp.maximum(most, count)

        @pl.when(most > 1)
        def _():
            for count, entry in zip(counts, done):

                def more(w, carry, entry=entry):
                    add(*window(entry, w))
                    return carry

                lax.fori_loop(1, count, more, 0)

        return carry

    lax.fori_loop(0, steps, layer_one, 0)

    parts = []
    for group in range(4):
        merged = None
        for sub in range(4):
            col = group * 4 + sub
            y, z = COLUMNS[col]
            row, b, c = (y >> 1) * 3 + (z >> 1), y & 1, z & 1
            local = lane8 & 31
            index = ((local >> 4) & 1) * 64 + (local & 1) * 32 + ((local >> 1) & 7) + b * 16 + c * 8
            got = lanes_of(table[3, row], index)
            merged = got if merged is None else jnp.where((lane8 >> 5) == sub, got, merged)
        parts.append(merged)
    species_row = jnp.concatenate(parts, axis=1)[0:1]
    node_t = sender_of(species_row)
    fv_t3 = three_weights(fv_ref[...].T, 1)
    square_t = jnp.zeros((128, 512), F32)
    for x in range(3):
        v3 = three(acc[1 + x, 0:512, :] * 0.25, 1)
        value = dot_t(fv_t3, v3)
        vec_t[x] = value
        square_t = square_t + value * value
        high, low = split(value)
        feat_t[0, 128 + x * 128 : 256 + x * 128, :] = high
        feat_t[1, 128 + x * 128 : 256 + x * 128, :] = low
    fs_t3 = three_weights(fs_ref[...].T, 1)
    fq_t3 = three_weights(fq_ref[...].T, 1)
    pre = dot_t(fs_t3, three(acc[0, 0:512, :] * 0.25, 1))
    pre = pre + dot(fs_t3, three(node_t, 0)) + dot(fq_t3, three(square_t, 0))
    scal_t, slope = silu_pair(pre)
    slope_t[...] = slope
    high, low = split(scal_t)
    feat_t[0, 0:128, :] = high
    feat_t[1, 0:128, :] = low
    scal_core = scal_t[:, 0:128]

    w_acc[...] = jnp.zeros((128, 128), F32)

    def layer_two(t, carry):
        hidden, _ = hidden_of(t, si_t3)
        weights = dot(so_t3, three(hidden, 0))
        pair = tile_rows(pair_buf, t)
        hot = onehot(pair[5:6], 512)
        feat = dot(feat_t[0], hot) + dot(feat_t[1], hot)
        saved_feat[t] = feat
        proj = pair[0:1] * feat[128:256] + pair[1:2] * feat[256:384] + pair[2:3] * feat[384:512]
        high, low = split(weights[0:128] * feat[0:128] + weights[128:256] * proj)
        member = onehot(pair[6:7], 128)
        w_acc[...] += dot_t(high, member) + dot_t(low, member)
        return carry

    lax.fori_loop(0, core_tiles, layer_two, 0)

    mixed = w_acc[...] * 0.25 + scal_core
    rs_col = jnp.broadcast_to(rs_ref[...], (128, 128)).T
    rf_col = jnp.broadcast_to(rf_ref[...], (128, 128)).T
    out, out_slope = silu_pair(dot(three_weights(sm_ref[...].T, 1), three(mixed, 0)))
    energy = jnp.sum(out * rs_col + scal_core * rf_col, axis=0, keepdims=True)
    index = (((lane8 >> 3) & 3) * 16 + (lane8 & 7)) * 2 + ((lane8 >> 5) & 1)
    index = jnp.where(lane8 < 64, ((lane8 >> 3) & 3) * 32 + (lane8 & 7) * 2 + ((lane8 >> 5) & 1), 0)
    energy_ref[...] = lanes_of(jnp.broadcast_to(energy, (8, 128)), index)[0:1, 0:64]

    mixed_grad = dot(three_weights(sm_ref[...], 1), three(rs_col * out_slope, 0))
    w_grad2 = jnp.concatenate(split(mixed_grad * 0.25), axis=1)
    feat_grad[...] = jnp.zeros((512, 512), F32)
    feat_grad[0:128, 0:128] = mixed_grad + rf_col

    def radial_back(t, slope, grad, outer3, inner3):
        high, low = split(grad)
        both = dot(outer3, high)
        hidden_grad = (both[0:64] + both[64:128] + dot(outer3[0:64], low)) * slope
        bes_grad = dot(inner3, three(hidden_grad, 0))[0:8]
        return jnp.sum(bes_grad * tile_rows(dbes_buf, t), axis=0, keepdims=True)

    def layer_two_back(t, carry):
        hidden, slope = hidden_of(t, si_t3)
        weights = dot(so_t3, three(hidden, 0))
        pair = tile_rows(pair_buf, t)
        feat = saved_feat[t]
        member = onehot(pair[6:7], 128)
        w_grad = dot(w_grad2, jnp.concatenate([member, member], axis=0))
        proj = pair[0:1] * feat[128:256] + pair[1:2] * feat[256:384] + pair[2:3] * feat[384:512]
        radial_grad = jnp.concatenate([w_grad * feat[0:128], w_grad * proj], axis=0)
        rho_grad = radial_back(t, slope, radial_grad, so_b3, si_b3)
        proj_grad = w_grad * weights[128:256]
        grads = [rho_grad]
        sends = [w_grad * weights[0:128]]
        for x in range(3):
            part = feat[128 + x * 128 : 256 + x * 128]
            grads.append(jnp.sum(proj_grad * part, axis=0, keepdims=True))
            sends.append(proj_grad * pair[x : x + 1])
        saved_pair_grad[t] = jnp.concatenate(grads + [jnp.zeros((4, TILE), F32)], axis=0)
        high, low = split(jnp.concatenate(sends, axis=0))
        hot = onehot(pair[5:6], 512)
        feat_grad[...] += dot_t(high, hot) + dot_t(low, hot)
        return carry

    lax.fori_loop(0, core_tiles, layer_two_back, 0)

    pre_grad3 = three(feat_grad[0:128, :] * slope_t[...], 0)
    m_grad = dot(three_weights(fs_ref[...], 1), pre_grad3)
    square_grad = dot(three_weights(fq_ref[...], 1), pre_grad3)
    fv_b3 = three_weights(fv_ref[...], 1)
    message_grads = [m_grad]
    for x in range(3):
        part = feat_grad[128 + x * 128 : 256 + x * 128, :] + 2.0 * vec_t[x] * square_grad
        message_grads.append(dot(fv_b3, three(part, 0)))
    for kind in range(4):
        high, low = split(message_grads[kind] * 0.25)
        for w in range(4):
            grad_lhs[w, kind * 128 : (kind + 1) * 128, 0:128] = high[:, w * 128 : (w + 1) * 128]
            grad_lhs[w, kind * 128 : (kind + 1) * 128, 128:256] = low[:, w * 128 : (w + 1) * 128]

    box_acc[...] = jnp.zeros((96, 128), F32)

    def layer_one_back(step, carry):
        group = []
        for part in range(UNROLL):
            t = step * UNROLL + part
            group.append((part, t, tile_rows(pair_buf, t), first_of(t) >> 7))

        def expanded(pair, w):
            member = onehot(pair[6:7] - (w * 128).astype(F32), 128)
            return dot(grad_lhs[w], jnp.concatenate([member, member], axis=0))

        for part, t, pair, first in group:
            expand[part] = expanded(pair, first)
        lasts = [
            jnp.where(t < tiles, (last_row[t] * 2 + 1) >> 7, 0)
            for _, t, _, _ in group
        ]
        crossing = lasts[0] > group[0][3]
        for last, entry in zip(lasts[1:], group[1:]):
            crossing = crossing | (last > entry[3])

        @pl.when(crossing)
        def _():
            for last, (part, t, pair, first) in zip(lasts, group):

                def more(w, carry, part=part, pair=pair):
                    expand[part] += expanded(pair, w)
                    return carry

                lax.fori_loop(first + 1, last + 1, more, 0)

        spreads = []
        for part, t, pair, first in group:
            sender = sender_of(pair[4:5])
            rg = saved_rg[t]
            v_grad = [expand[part, 128 + x * 128 : 256 + x * 128, :] for x in range(3)]
            along = pair[0:1] * v_grad[0] + pair[1:2] * v_grad[1] + pair[2:3] * v_grad[2]
            radial_grad = jnp.concatenate(
                [expand[part, 0:128, :] * sender, along * sender], axis=0
            )
            earlier = saved_pair_grad[t]
            rho_grad = radial_back(t, saved_slope[t], radial_grad, fo_b3, fi_b3) + earlier[0:1]
            unit_grad = [
                jnp.sum(rg * v_grad[x], axis=0, keepdims=True) + earlier[1 + x : 2 + x]
                for x in range(3)
            ]
            unit = [pair[x : x + 1] for x in range(3)]
            inner = unit[0] * unit_grad[0] + unit[1] * unit_grad[1] + unit[2] * unit_grad[2]
            inv = pair[3:4]
            values = []
            for x in range(3):
                value = (unit_grad[x] - unit[x] * inner) * inv + rho_grad * unit[x]
                high = value.astype(BF16).astype(F32)
                values += [high, value - high]
            both = pair[7:8].astype(I32)
            for code, sign in ((both >> 11, 1.0), (both & 2047, -1.0)):
                row = jnp.broadcast_to(code >> 7, (16, TILE)) == iota((16, TILE), 0)
                stack = [jnp.where(row, sign * value, 0.0) for value in values]
                lane = jnp.where(iota((128, TILE), 0) == (code & 127), 1.0, 0.0).astype(BF16)
                spreads.append(dot_t(jnp.concatenate(stack, axis=0).astype(BF16), lane))
        box_acc[...] += sum(spreads[1:], spreads[0])
        return carry

    lax.fori_loop(0, steps, layer_one_back, 0)

    for comp in range(3):
        grid = box_acc[comp * 32 : comp * 32 + 16, :] + box_acc[comp * 32 + 16 : comp * 32 + 32, :]
        for dz, ref in ((-1, down_ref), (0, mid_ref), (1, up_ref)):
            for dy in range(3):
                row = dy * 3 + dz + 1
                ref[dy, comp : comp + 1, :] = grid[row : row + 1, :]
    for ref in (down_ref, mid_ref, up_ref):
        for dy in range(3):
            ref[dy, 3:8, :] = jnp.zeros((5, 128), F32)


def pair_program(own, low, high, weights):
    vm = pltpu.VMEM
    pair_rows = (MAX_TILES * 2 + 6) * 8
    scratch = [
        vm((5, 9, 8, 128), F32),
        vm((256, 128), F32),
        vm((32, 8, 128), F32),
        vm((5, 256, 128), F32),
        vm((256, 128), F32),
        vm((2048, 128), F32),
        vm((pair_rows, 128), F32),
        vm((pair_rows, 128), F32),
        vm((pair_rows, 128), F32),
        vm((pair_rows, 128), F32),
        vm((8, 512), I32),
        pltpu.SMEM((8, 512), I32),
        pltpu.SMEM((256,), I32),
        pltpu.SemaphoreType.DMA,
        vm((4, 512 + WINDOW, 128), F32),
        vm((3, 128, 512), F32),
        vm((128, 512), F32),
        vm((2, 512, 512), BF16),
        vm((512, 512), F32),
        vm((128, 128), F32),
        vm((4, 512, 256), BF16),
        vm((UNROLL, 512, TILE), F32),
        vm((MAX_TILES, 128, TILE), F32),
        vm((MAX_TILES, 64, TILE), F32),
        vm((MAX_CORE_TILES, 512, TILE), F32),
        vm((MAX_TILES, 8, TILE), F32),
        vm((96, 128), F32),
        vm((128, 128), F32),
    ]
    whole = pl.BlockSpec(memory_space=pltpu.VMEM)
    piece = jax.ShapeDtypeStruct((3, 8, 128), F32)
    return pl.pallas_call(
        main_kernel,
        out_shape=(jax.ShapeDtypeStruct((1, 64), F32), piece, piece, piece),
        in_specs=[whole] * (3 + len(weights)),
        out_specs=(whole,) * 4,
        scratch_shapes=scratch,
        compiler_params=pltpu.CompilerParams(vmem_limit_bytes=60 * 1024 * 1024),
        interpret=INTERPRET,
    )(own, low, high, *weights)


def pack(positions, species, counts, neighbors):
    whole = pl.BlockSpec(memory_space=pltpu.VMEM)
    return pl.pallas_call(
        pack_kernel,
        out_shape=jax.ShapeDtypeStruct((5, 8, 128), F32),
        in_specs=[whole] * 4,
        out_specs=whole,
        interpret=INTERPRET,
    )(positions, species.reshape(1, 64), counts.reshape(1, 64), neighbors)


def join_y(own, below, above):
    return jnp.concatenate(
        [below[2:5], below[7:10], own, above[0:2], above[4:7], above[9:10]], axis=0
    )


def ring(axis, step):
    count = lax.axis_size(axis)
    return [(i, (i + step) % count) for i in range(count)]


def shards(
    positions,
    species,
    neighbors,
    neighbor_counts,
    embedding,
    first_inner,
    first_outer,
    first_scalar,
    first_vector,
    first_square,
    second_inner,
    second_outer,
    second_mix,
    readout_first,
    readout_second,
):
    packed = pack(positions, species, neighbor_counts, neighbors)
    partner = lax.ppermute(packed, "gx", ring("gx", 1))
    both = jnp.concatenate([packed, partner], axis=0)
    below = lax.ppermute(both, "gy", ring("gy", 1))
    above = lax.ppermute(both, "gy", ring("gy", -1))
    layer = join_y(both, below, above)
    low = lax.ppermute(layer, "gz", ring("gz", 1))
    high = lax.ppermute(layer, "gz", ring("gz", -1))
    weights = (
        embedding,
        first_inner,
        first_outer,
        first_scalar,
        first_vector,
        first_square,
        second_inner,
        second_outer,
        second_mix,
        readout_first.reshape(1, 128),
        readout_second.reshape(1, 128),
    )
    energy, up, mid, down = pair_program(layer, low, high, weights)
    folded = mid + lax.ppermute(up, "gz", ring("gz", 1)) + lax.ppermute(down, "gz", ring("gz", -1))
    total = folded[1] + lax.ppermute(folded[2], "gy", ring("gy", 1))
    total = total + lax.ppermute(folded[0], "gy", ring("gy", -1))
    return (energy.reshape(64), -total[0:3, 0:64])


def solution(mesh):
    spread = ("gx", "gy", "gz")
    placed = (P(None, spread), P(spread), P(spread, None), P(spread)) + (P(),) * 11
    return jax.shard_map(
        shards,
        mesh=mesh,
        in_specs=placed,
        out_specs=(P(spread), P(None, spread)),
        check_vma=False,
    )
```

```python
import functools

import jax
import jax.numpy as jnp
from jax import lax
from jax.experimental import pallas as pl
from jax.experimental.pallas import tpu as pltpu
from jax.sharding import PartitionSpec as P

F32 = jnp.float32
BF16 = jnp.bfloat16
I32 = jnp.int32
TILE = 256
MAX_TILES = 129
MAX_CORE_TILES = 32
WINDOW = 64
UNROLL = 3
KEPT_TILES = 30
INTERPRET = False

COLUMNS = [
    (1 + ((col >> 3) * 2 + ((col >> 1) & 1) + 1) % 4, 1 + (((col >> 2) & 1) * 2 + (col & 1) + 1) % 4)
    for col in range(16)
]
LIST_BASE = {1: 0, 2: 6, 3: 8, 4: 16}
LIST_STEP = {1: 3, 2: 5, 3: 5, 4: 3}
COORD_BASE = {-1: 2, 0: 10, 1: 18}
COORD_STEP = {-1: 3, 0: 5, 1: 3}


def split(x):
    high = x.astype(BF16)
    return high, (x - high.astype(F32)).astype(BF16)


def three(x, axis):
    high, low = split(x)
    return jnp.concatenate([high, low, high], axis=axis)


def three_weights(w, axis):
    high, low = split(w)
    return jnp.concatenate([high, high, low], axis=axis)


def dot(a, b):
    return lax.dot_general(a, b, (((1,), (0,)), ((), ())), preferred_element_type=F32)


def dot_t(a, b):
    return lax.dot_general(a, b, (((1,), (1,)), ((), ())), preferred_element_type=F32)


def lanes_of(table, index):
    return jnp.take_along_axis(table, index, axis=1, mode="promise_in_bounds")


def silu_pair(x):
    gate = 1.0 / (1.0 + jnp.exp(-x))
    value = x * gate
    return value, gate + value * (1.0 - gate)


def pack_kernel(pos_ref, species_ref, counts_ref, neighbors_ref, out_ref):
    ids = neighbors_ref[...].astype(F32)
    joined = jnp.concatenate([ids[:32], ids[32:]], axis=1)
    for part in range(4):
        out_ref[part] = joined[part * 8 : part * 8 + 8]
    rows = jnp.concatenate(
        [
            pos_ref[...],
            species_ref[...].astype(F32),
            counts_ref[...].astype(F32),
            jnp.zeros((3, 64), F32),
        ],
        axis=0,
    )
    out_ref[4] = jnp.concatenate([rows, rows], axis=1)


def iota(shape, axis):
    return lax.broadcasted_iota(I32, shape, axis)


def main_kernel(
    own_ref,
    low_ref,
    high_ref,
    emb_ref,
    fi_ref,
    fo_ref,
    fs_ref,
    fv_ref,
    fq_ref,
    si_ref,
    so_ref,
    sm_ref,
    rf_ref,
    rs_ref,
    energy_ref,
    up_ref,
    mid_ref,
    down_ref,
    table,
    mask_buf,
    lists,
    raw,
    counted_buf,
    rowbuf,
    buf,
    bes_buf,
    dbes_buf,
    pair_buf,
    offs_vmem,
    offs,
    last_row,
    sem,
    acc,
    vec_t,
    slope_t,
    feat_t,
    feat_grad,
    w_acc,
    grad_lhs,
    expand,
    saved,
    saved_core,
    saved_pair_grad,
    box_acc,
    emb_pad,
):
    lane8 = iota((8, 128), 1)
    sub8 = iota((8, 128), 0)
    upper = lane8 >= 64
    layer_refs = {-1: low_ref, 0: own_ref, 1: high_ref}

    for dy in (-1, 0, 1):
        for dz in (-1, 0, 1):
            ref = layer_refs[dz]
            base = COORD_BASE[dy]
            joined = jnp.where(upper, ref[base + COORD_STEP[dy]], ref[base])
            shift_x = jnp.where(upper, 12.0, 0.0)
            shift = jnp.where(
                sub8 == 0, shift_x, jnp.where(sub8 == 1, 12.0 * dy, jnp.where(sub8 == 2, 12.0 * dz, 0.0))
            )
            joined = joined + shift
            row = (dy + 1) * 3 + dz + 1
            for comp in range(5):
                table[comp, row] = jnp.broadcast_to(joined[comp : comp + 1], (8, 128))

    for col, (y, z) in enumerate(COLUMNS):
        layer = layer_refs[(z >> 1) - 1]
        for xd in range(2):
            lists[col * 2 + xd] = layer[LIST_BASE[y] + xd * LIST_STEP[y] + (z & 1)]

    def place_of(part):
        col, xd = part >> 1, part & 1
        y = 1 + (((col >> 3) * 2 + ((col >> 1) & 1) + 1) & 3)
        z = 1 + ((((col >> 2) & 1) * 2 + (col & 1) + 1) & 3)
        lane = xd * 64 + (y & 1) * 16 + (z & 1) * 8
        return y, z, xd, (y >> 1) * 3 + (z >> 1), lane

    def distances(part, carry):
        y, z, xd, row_l, base_l = place_of(part)
        y_low = jnp.where(y >= 3, 1, 0)
        z_low = jnp.where(z >= 3, 1, 0)
        row0 = y_low * 3 + z_low
        tile = lists[part].astype(I32)
        r1 = ((tile >> 3) & 3) + 1
        q1 = ((tile >> 5) & 3) + 1
        p1 = ((tile >> 7) & 3) + 1
        x_side = (1 - ((p1 >> 1) & 1)) ^ xd
        y_index = (q1 >> 1) + ((y >> 1) - 1 - y_low)
        z_index = (r1 >> 1) + ((z >> 1) - 1 - z_low)
        lane = x_side * 64 + (p1 & 1) * 32 + (q1 & 1) * 16 + (r1 & 1) * 8 + (tile & 7)
        lane_l = jnp.where(upper, 32, 0) + sub8 + base_l
        y_zero = y_index == 0
        z_zero = z_index == 0

        def fetch(comp):
            low = jnp.where(
                z_zero, lanes_of(table[comp, row0], lane), lanes_of(table[comp, row0 + 1], lane)
            )
            top = jnp.where(
                z_zero, lanes_of(table[comp, row0 + 3], lane), lanes_of(table[comp, row0 + 4], lane)
            )
            return jnp.where(y_zero, low, top)

        d = [fetch(comp) - lanes_of(table[comp, row_l], lane_l) for comp in range(3)]
        d[0] = jnp.where(d[0] > 12.0, d[0] - 24.0, jnp.where(d[0] < -12.0, d[0] + 24.0, d[0]))
        species = fetch(3)
        count = lanes_of(table[4, row_l], lane_l)
        square = d[0] * d[0] + d[1] * d[1] + d[2] * d[2] + 0.25
        slot = (lane8 & 63).astype(F32)
        reach = (square < 36.0) & (slot < count)
        inside = ((y_index >> 1) == 0) & ((z_index >> 1) == 0)
        live = jnp.where(reach & inside, 1.0, 0.0)
        code = (row0 + y_index * 3 + z_index) * 128 + lane
        rows = pl.ds(pl.multiple_of(part * 8, 8), 8)
        mask_buf[rows, :] = live
        raw[0, rows, :] = d[0]
        raw[1, rows, :] = d[1]
        raw[2, rows, :] = d[2]
        raw[3, rows, :] = species
        raw[4, rows, :] = code.astype(F32)
        return carry

    lax.fori_loop(0, 32, distances, 0, unroll=4)

    mask = mask_buf[...].astype(BF16)
    upto = jnp.where(iota((128, 128), 0) <= iota((128, 128), 1), 1.0, 0.0).astype(BF16)
    within = dot(mask, upto)
    totals = dot_t(jnp.ones((8, 128), BF16), mask)
    before = jnp.where(iota((256, 256), 0) < iota((256, 256), 1), 1.0, 0.0).astype(BF16)
    starts = dot(totals.astype(BF16), before)
    offs_vmem[:, 0:256] = starts.astype(I32)
    offs_vmem[:, 256:512] = totals.astype(I32)
    copy = pltpu.make_async_copy(offs_vmem, offs, sem)
    copy.start()

    counted_buf[...] = within

    def to_front(part, carry):
        _, _, _, row_l, base_l = place_of(part)
        at = pl.multiple_of(part * 8, 8)
        rows = pl.ds(at, 8)
        counted = counted_buf[rows, :]
        wanted = (lane8 + 1).astype(F32)
        place = jnp.zeros((8, 128), I32)
        for step in (64, 32, 16, 8, 4, 2, 1):
            probe = lanes_of(counted, place + (step - 1))
            place = jnp.where(probe < wanted, place + step, place)
        half = jnp.where(place >= 64, 1, 0)
        atom = (at + sub8) * 2 + half
        code_l = row_l * 128 + base_l + sub8 + half * 32
        fields = [lanes_of(raw[k, rows, :], place) for k in range(5)]
        fields += [atom.astype(F32), code_l.astype(F32)]
        for k, field in enumerate(fields):
            rowbuf[pl.ds(at * 8 + k, 8, stride=8), :] = field
        return carry

    lax.fori_loop(0, 32, to_front, 0, unroll=16)

    copy.wait()

    def join_row(r, current):
        start = offs[0, r]
        length = offs[0, 256 + r]
        shift = start & 127
        rolled = pltpu.roll(rowbuf[pl.ds(r * 8, 8), :], shift, 1)
        current = jnp.where(lane8 >= shift, rolled, current)
        buf[pl.ds((start >> 7) * 8, 8), :] = current
        last_row[start >> 8] = r
        return jnp.where(shift + length >= 128, rolled, current)

    current = lax.fori_loop(0, 256, join_row, jnp.zeros((8, 128), F32), unroll=16)
    total = offs[0, 255] + offs[0, 511]
    core_total = offs[0, 64]
    buf[pl.ds((total >> 7) * 8, 8), :] = current
    last_row[jnp.maximum(total - 1, 0) >> 8] = 255
    tiles = (total + (TILE - 1)) // TILE
    core_tiles = (core_total + (TILE - 1)) // TILE
    steps = (tiles + UNROLL - 1) // UNROLL

    def basis(chunk, carry):
        at = chunk * 64
        field = [buf[pl.ds(at + k, 8, stride=8), :] for k in range(7)]
        valid = (chunk * 1024 + sub8 * 128 + lane8) < total
        d = [jnp.where(valid, field[k], 100.0) for k in range(3)]
        species = jnp.where(valid, field[3], 0.0)
        code = jnp.where(valid, field[4], 0.0).astype(I32)
        atom = jnp.where(valid, field[5], -1.0)
        code_l = jnp.where(valid, field[6], 0.0)
        square = d[0] * d[0] + d[1] * d[1] + d[2] * d[2] + 0.25
        rho = jnp.sqrt(square)
        inv = 1.0 / rho
        t = jnp.where(rho < 6.0, rho * (1.0 / 6.0), 1.0)
        inside = valid & (rho < 6.0)
        angle = t * 3.14159265358979 - 1.5707963267948966
        a2 = angle * angle
        sin_a = angle * (
            1.0
            + a2
            * (
                -1.0 / 6
                + a2
                * (
                    1.0 / 120
                    + a2 * (-1.0 / 5040 + a2 * (1.0 / 362880 + a2 * (-1.0 / 39916800 + a2 / 6227020800.0)))
                )
            )
        )
        cos_a = 1.0 + a2 * (
            -0.5
            + a2
            * (
                1.0 / 24
                + a2
                * (
                    -1.0 / 720
                    + a2
                    * (1.0 / 40320 + a2 * (-1.0 / 3628800 + a2 * (1.0 / 479001600 - a2 / 87178291200.0)))
                )
            )
        )
        sine, cosine = cos_a, -sin_a
        t2 = t * t
        t5 = t2 * t2 * t
        f = 1.0 + t5 * t * (-28.0 + t * (48.0 - 21.0 * t))
        f = jnp.where(inside, f, 0.0)
        one = 1.0 - t
        df = jnp.where(inside, -28.0 * t5 * one * one, 0.0)
        scale = 0.5773502691896258
        amount = scale * inv * f
        slope = scale * inv * (df - inv * f)
        s_prev, c_prev = jnp.zeros((8, 128), F32), jnp.ones((8, 128), F32)
        s_now, c_now = sine, cosine
        for n in range(8):
            bes_buf[pl.ds(at + n, 8, stride=8), :] = s_now * amount
            dbes_buf[pl.ds(at + n, 8, stride=8), :] = (
                c_now * amount * ((n + 1) * 0.5235987755982988) + s_now * slope
            )
            s_now, s_prev = 2.0 * cosine * s_now - s_prev, s_now
            c_now, c_prev = 2.0 * cosine * c_now - c_prev, c_now
        row = code >> 7
        lane = code & 127
        row_y = jnp.where(row >= 6, 2, jnp.where(row >= 3, 1, 0))
        row_z = row - 3 * row_y
        y = row_y * 2 + ((lane >> 4) & 1) - 1
        z = row_z * 2 + ((lane >> 3) & 1) - 1
        near = (y >= 0) & (y < 4) & (z >= 0) & (z < 4)
        y = (y + 3) & 3
        z = (z + 3) & 3
        column = (y >> 1) * 8 + (z >> 1) * 4 + (y & 1) * 2 + (z & 1)
        source = column * 32 + ((lane >> 6) & 1) * 16 + (lane & 7) * 2 + ((lane >> 5) & 1)
        source = jnp.where(near, source, -1)
        both = code.astype(F32) * 2048.0 + code_l
        kept = [d[0] * inv, d[1] * inv, d[2] * inv, inv, species, source.astype(F32), atom, both]
        for k, value in enumerate(kept):
            pair_buf[pl.ds(at + k, 8, stride=8), :] = value
        return carry

    lax.fori_loop(0, (steps * UNROLL * TILE + 1023) // 1024, basis, 0)

    fi3 = jnp.concatenate([fi_ref[...], jnp.zeros((24, 64), F32)], axis=0)
    si3 = jnp.concatenate([si_ref[...], jnp.zeros((24, 64), F32)], axis=0)

    def inner_weights(padded):
        w = padded.T[:, 0:8]
        high = w.astype(BF16).astype(F32)
        low = w - high
        return jnp.concatenate([high, high, low, jnp.zeros((64, 8), F32)], axis=1).astype(BF16)

    fi_t3 = inner_weights(fi3)
    si_t3 = inner_weights(si3)
    fo_t3 = three_weights(fo_ref[...].T, 1)
    so_t3 = three_weights(so_ref[...].T, 1)
    emb_pad[...] = jnp.zeros((128, 128), F32)
    emb_pad[0:89, :] = emb_ref[...]
    emb_t2 = jnp.concatenate(split(emb_pad[...].T), axis=1)

    def tile_rows(ref, t):
        at = t * 16
        return jnp.concatenate([ref[pl.ds(at, 8), :], ref[pl.ds(at + 8, 8), :]], axis=1)

    def stacked(ref, t):
        rows = tile_rows(ref, t)
        high = rows.astype(BF16).astype(F32)
        stack = jnp.concatenate([high, rows - high, high, jnp.zeros((8, TILE), F32)], axis=0)
        return stack.astype(BF16)

    def radial_of(t, inner, outer):
        hidden, slope = silu_pair(dot(inner, stacked(bes_buf, t)))
        rate = dot(inner, stacked(dbes_buf, t)) * slope
        return dot(outer, three(hidden, 0)), dot(outer, three(rate, 0))

    def onehot(index_row, rows):
        hit = iota((rows, index_row.shape[1]), 0) == index_row.astype(I32)
        return jnp.where(hit, 1.0, 0.0).astype(BF16)

    def sender_of(species_row):
        hot = onehot(species_row, 128)
        return dot(emb_t2, jnp.concatenate([hot, hot], axis=0))

    def first_of(t):
        before = jnp.clip(t - 1, 0, jnp.maximum(tiles - 1, 0))
        return jnp.where(t == 0, 0, last_row[before]) * 2

    acc[...] = jnp.zeros(acc.shape, F32)

    def first_terms(t):
        weights, rates = radial_of(t, fi_t3, fo_t3)
        pair = tile_rows(pair_buf, t)
        sender = sender_of(pair[4:5])
        message = weights[0:128] * sender
        rg = weights[128:256] * sender
        return pair, message, rg, rates[0:128] * sender, rates[128:256] * sender

    def layer_one(step, carry):
        done = []
        for part in range(UNROLL):
            t = step * UNROLL + part
            pair, message, rg, rate_0, rate_1 = first_terms(t)
            kept = jnp.minimum(t, KEPT_TILES)
            saved[kept, 0:128, :] = rg
            saved[kept, 128:256, :] = rate_0
            saved[kept, 256:384, :] = rate_1
            saved_pair_grad[t] = jnp.zeros((8, TILE), F32)
            done.append((t, first_of(t) & -8, pair, split(message), split(rg)))

        def window(entry, w):
            _, base, pair, (m_high, m_low), (v_high, v_low) = entry
            at = base + w * WINDOW
            unit = [split(pair[k : k + 1]) for k in range(3)]
            hot = onehot(pair[6:7] - at.astype(F32), WINDOW)
            u_high = jnp.concatenate([hot * high for high, _ in unit], axis=0)
            u_low = jnp.concatenate([hot * low for _, low in unit], axis=0)
            m = dot_t(hot, m_high) + dot_t(hot, m_low)
            v = dot_t(u_high, v_high) + dot_t(u_high, v_low) + dot_t(u_low, v_high)
            return pl.ds(pl.multiple_of(at, 8), WINDOW), m, v

        def add(rows, m, v):
            acc[0, rows, :] += m
            for x in range(3):
                acc[1 + x, rows, :] += v[x * WINDOW : (x + 1) * WINDOW]

        for sums in [window(entry, 0) for entry in done]:
            add(*sums)
        counts = [
            jnp.where(t < tiles, (last_row[t] * 2 + 1 - base) // WINDOW + 1, 1)
            for t, base, _, _, _ in done
        ]
        most = counts[0]
        for count in counts[1:]:
            most = jnp.maximum(most, count)

        @pl.when(most > 1)
        def _():
            for count, entry in zip(counts, done):

                def more(w, carry, entry=entry):
                    add(*window(entry, w))
                    return carry

                lax.fori_loop(1, count, more, 0)

        return carry

    lax.fori_loop(0, steps, layer_one, 0)

    parts = []
    for group in range(4):
        merged = None
        for sub in range(4):
            col = group * 4 + sub
            y, z = COLUMNS[col]
            row, b, c = (y >> 1) * 3 + (z >> 1), y & 1, z & 1
            local = lane8 & 31
            index = ((local >> 4) & 1) * 64 + (local & 1) * 32 + ((local >> 1) & 7) + b * 16 + c * 8
            got = lanes_of(table[3, row], index)
            merged = got if merged is None else jnp.where((lane8 >> 5) == sub, got, merged)
        parts.append(merged)
    species_row = jnp.concatenate(parts, axis=1)[0:1]
    node_t = sender_of(species_row)
    fv_t3 = three_weights(fv_ref[...].T, 1)
    square_t = jnp.zeros((128, 512), F32)
    for x in range(3):
        v3 = three(acc[1 + x, 0:512, :] * 0.25, 1)
        value = dot_t(fv_t3, v3)
        vec_t[x] = value
        square_t = square_t + value * value
        high, low = split(value)
        feat_t[0, 128 + x * 128 : 256 + x * 128, :] = high
        feat_t[1, 128 + x * 128 : 256 + x * 128, :] = low
    fs_t3 = three_weights(fs_ref[...].T, 1)
    fq_t3 = three_weights(fq_ref[...].T, 1)
    pre = dot_t(fs_t3, three(acc[0, 0:512, :] * 0.25, 1))
    pre = pre + dot(fs_t3, three(node_t, 0)) + dot(fq_t3, three(square_t, 0))
    scal_t, slope = silu_pair(pre)
    slope_t[...] = slope
    high, low = split(scal_t)
    feat_t[0, 0:128, :] = high
    feat_t[1, 0:128, :] = low
    scal_core = scal_t[:, 0:128]

    w_acc[...] = jnp.zeros((128, 128), F32)

    def layer_two(t, carry):
        weights, rates = radial_of(t, si_t3, so_t3)
        pair = tile_rows(pair_buf, t)
        hot = onehot(pair[5:6], 512)
        feat = dot(feat_t[0], hot) + dot(feat_t[1], hot)
        proj = pair[0:1] * feat[128:256] + pair[1:2] * feat[256:384] + pair[2:3] * feat[384:512]
        saved_core[t, 0:384, :] = feat[128:512]
        saved_core[t, 384:640, :] = weights
        saved_core[t, 640:768, :] = rates[0:128] * feat[0:128] + rates[128:256] * proj
        high, low = split(weights[0:128] * feat[0:128] + weights[128:256] * proj)
        member = onehot(pair[6:7], 128)
        w_acc[...] += dot_t(high, member) + dot_t(low, member)
        return carry

    lax.fori_loop(0, core_tiles, layer_two, 0)

    mixed = w_acc[...] * 0.25 + scal_core
    rs_col = jnp.broadcast_to(rs_ref[...], (128, 128)).T
    rf_col = jnp.broadcast_to(rf_ref[...], (128, 128)).T
    out, out_slope = silu_pair(dot(three_weights(sm_ref[...].T, 1), three(mixed, 0)))
    energy = jnp.sum(out * rs_col + scal_core * rf_col, axis=0, keepdims=True)
    index = (((lane8 >> 3) & 3) * 16 + (lane8 & 7)) * 2 + ((lane8 >> 5) & 1)
    index = jnp.where(lane8 < 64, ((lane8 >> 3) & 3) * 32 + (lane8 & 7) * 2 + ((lane8 >> 5) & 1), 0)
    energy_ref[...] = lanes_of(jnp.broadcast_to(energy, (8, 128)), index)[0:1, 0:64]

    mixed_grad = dot(three_weights(sm_ref[...], 1), three(rs_col * out_slope, 0))
    w_grad2 = jnp.concatenate(split(mixed_grad * 0.25), axis=1)
    feat_grad[...] = jnp.zeros((512, 512), F32)
    feat_grad[0:128, 0:128] = mixed_grad + rf_col

    def layer_two_back(t, carry):
        pair = tile_rows(pair_buf, t)
        member = onehot(pair[6:7], 128)
        w_grad = dot(w_grad2, jnp.concatenate([member, member], axis=0))
        proj_grad = w_grad * saved_core[t, 512:640, :]
        grads = [jnp.sum(w_grad * saved_core[t, 640:768, :], axis=0, keepdims=True)]
        sends = [w_grad * saved_core[t, 384:512, :]]
        for x in range(3):
            part = saved_core[t, x * 128 : 128 + x * 128, :]
            grads.append(jnp.sum(proj_grad * part, axis=0, keepdims=True))
            sends.append(proj_grad * pair[x : x + 1])
        saved_pair_grad[t] = jnp.concatenate(grads + [jnp.zeros((4, TILE), F32)], axis=0)
        high, low = split(jnp.concatenate(sends, axis=0))
        hot = onehot(pair[5:6], 512)
        feat_grad[...] += dot_t(high, hot) + dot_t(low, hot)
        return carry

    lax.fori_loop(0, core_tiles, layer_two_back, 0)

    pre_grad3 = three(feat_grad[0:128, :] * slope_t[...], 0)
    m_grad = dot(three_weights(fs_ref[...], 1), pre_grad3)
    square_grad = dot(three_weights(fq_ref[...], 1), pre_grad3)
    fv_b3 = three_weights(fv_ref[...], 1)
    message_grads = [m_grad]
    for x in range(3):
        part = feat_grad[128 + x * 128 : 256 + x * 128, :] + 2.0 * vec_t[x] * square_grad
        message_grads.append(dot(fv_b3, three(part, 0)))
    for kind in range(4):
        high, low = split(message_grads[kind] * 0.25)
        for w in range(4):
            grad_lhs[w, kind * 128 : (kind + 1) * 128, 0:128] = high[:, w * 128 : (w + 1) * 128]
            grad_lhs[w, kind * 128 : (kind + 1) * 128, 128:256] = low[:, w * 128 : (w + 1) * 128]

    box_acc[...] = jnp.zeros((96, 128), F32)

    def layer_one_back(step, carry, again):
        group = []
        for part in range(UNROLL):
            t = step * UNROLL + part
            group.append((part, t, tile_rows(pair_buf, t), first_of(t) >> 7))

        def expanded(pair, w):
            member = onehot(pair[6:7] - (w * 128).astype(F32), 128)
            return dot(grad_lhs[w], jnp.concatenate([member, member], axis=0))

        for part, t, pair, first in group:
            expand[part] = expanded(pair, first)
        lasts = [
            jnp.where(t < tiles, (last_row[t] * 2 + 1) >> 7, 0)
            for _, t, _, _ in group
        ]
        crossing = lasts[0] > group[0][3]
        for last, entry in zip(lasts[1:], group[1:]):
            crossing = crossing | (last > entry[3])

        @pl.when(crossing)
        def _():
            for last, (part, t, pair, first) in zip(lasts, group):

                def more(w, carry, part=part, pair=pair):
                    expand[part] += expanded(pair, w)
                    return carry

                lax.fori_loop(first + 1, last + 1, more, 0)

        spreads = []
        for part, t, pair, first in group:
            if again:
                _, _, rg, rate_0, rate_1 = first_terms(t)
            else:
                rg, rate_0, rate_1 = (saved[t, k * 128 : k * 128 + 128, :] for k in range(3))
            earlier = saved_pair_grad[t]
            rho_grad = earlier[0:1] + jnp.sum(expand[part, 0:128, :] * rate_0, axis=0, keepdims=True)
            unit_grad = []
            for x in range(3):
                v_grad = expand[part, 128 + x * 128 : 256 + x * 128, :]
                along = jnp.sum(v_grad * rate_1, axis=0, keepdims=True)
                rho_grad = rho_grad + pair[x : x + 1] * along
                across = jnp.sum(v_grad * rg, axis=0, keepdims=True)
                unit_grad.append(across + earlier[1 + x : 2 + x])
            unit = [pair[x : x + 1] for x in range(3)]
            inner = unit[0] * unit_grad[0] + unit[1] * unit_grad[1] + unit[2] * unit_grad[2]
            inv = pair[3:4]
            values = []
            for x in range(3):
                value = (unit_grad[x] - unit[x] * inner) * inv + rho_grad * unit[x]
                high = value.astype(BF16).astype(F32)
                values += [high, value - high]
            both = pair[7:8].astype(I32)
            for code, sign in ((both >> 11, 1.0), (both & 2047, -1.0)):
                row = jnp.broadcast_to(code >> 7, (16, TILE)) == iota((16, TILE), 0)
                stack = [jnp.where(row, sign * value, 0.0) for value in values]
                lane = onehot(code & 127, 128)
                spreads.append(dot_t(jnp.concatenate(stack, axis=0).astype(BF16), lane))
        box_acc[...] += sum(spreads[1:], spreads[0])
        return carry

    kept_steps = jnp.minimum(steps, KEPT_TILES // UNROLL)
    lax.fori_loop(0, kept_steps, functools.partial(layer_one_back, again=False), 0)
    lax.fori_loop(kept_steps, steps, functools.partial(layer_one_back, again=True), 0)

    for comp in range(3):
        grid = box_acc[comp * 32 : comp * 32 + 16, :] + box_acc[comp * 32 + 16 : comp * 32 + 32, :]
        for dz, ref in ((-1, down_ref), (0, mid_ref), (1, up_ref)):
            for dy in range(3):
                row = dy * 3 + dz + 1
                ref[dy, comp : comp + 1, :] = grid[row : row + 1, :]
    for ref in (down_ref, mid_ref, up_ref):
        for dy in range(3):
            ref[dy, 3:8, :] = jnp.zeros((5, 128), F32)


def pair_program(own, low, high, weights):
    vm = pltpu.VMEM
    pair_rows = (MAX_TILES * 2 + 6) * 8
    scratch = [
        vm((5, 9, 8, 128), F32),
        vm((256, 128), F32),
        vm((32, 8, 128), F32),
        vm((5, 256, 128), F32),
        vm((256, 128), F32),
        vm((2048, 128), F32),
        vm((pair_rows, 128), F32),
        vm((pair_rows, 128), F32),
        vm((pair_rows, 128), F32),
        vm((pair_rows, 128), F32),
        vm((8, 512), I32),
        pltpu.SMEM((8, 512), I32),
        pltpu.SMEM((256,), I32),
        pltpu.SemaphoreType.DMA,
        vm((4, 512 + WINDOW, 128), F32),
        vm((3, 128, 512), F32),
        vm((128, 512), F32),
        vm((2, 512, 512), BF16),
        vm((512, 512), F32),
        vm((128, 128), F32),
        vm((4, 512, 256), BF16),
        vm((UNROLL, 512, TILE), F32),
        vm((KEPT_TILES + 1, 384, TILE), F32),
        vm((MAX_CORE_TILES, 768, TILE), F32),
        vm((MAX_TILES, 8, TILE), F32),
        vm((96, 128), F32),
        vm((128, 128), F32),
    ]
    whole = pl.BlockSpec(memory_space=pltpu.VMEM)
    piece = jax.ShapeDtypeStruct((3, 8, 128), F32)
    return pl.pallas_call(
        main_kernel,
        out_shape=(jax.ShapeDtypeStruct((1, 64), F32), piece, piece, piece),
        in_specs=[whole] * (3 + len(weights)),
        out_specs=(whole,) * 4,
        scratch_shapes=scratch,
        compiler_params=pltpu.CompilerParams(vmem_limit_bytes=60 * 1024 * 1024),
        interpret=INTERPRET,
    )(own, low, high, *weights)


def pack(positions, species, counts, neighbors):
    whole = pl.BlockSpec(memory_space=pltpu.VMEM)
    return pl.pallas_call(
        pack_kernel,
        out_shape=jax.ShapeDtypeStruct((5, 8, 128), F32),
        in_specs=[whole] * 4,
        out_specs=whole,
        interpret=INTERPRET,
    )(positions, species.reshape(1, 64), counts.reshape(1, 64), neighbors)


def join_y(own, below, above):
    return jnp.concatenate(
        [below[2:5], below[7:10], own, above[0:2], above[4:7], above[9:10]], axis=0
    )


def ring(axis, step):
    count = lax.axis_size(axis)
    return [(i, (i + step) % count) for i in range(count)]


def shards(
    positions,
    species,
    neighbors,
    neighbor_counts,
    embedding,
    first_inner,
    first_outer,
    first_scalar,
    first_vector,
    first_square,
    second_inner,
    second_outer,
    second_mix,
    readout_first,
    readout_second,
):
    packed = pack(positions, species, neighbor_counts, neighbors)
    partner = lax.ppermute(packed, "gx", ring("gx", 1))
    both = jnp.concatenate([packed, partner], axis=0)
    below = lax.ppermute(both, "gy", ring("gy", 1))
    above = lax.ppermute(both, "gy", ring("gy", -1))
    layer = join_y(both, below, above)
    low = lax.ppermute(layer, "gz", ring("gz", 1))
    high = lax.ppermute(layer, "gz", ring("gz", -1))
    weights = (
        embedding,
        first_inner,
        first_outer,
        first_scalar,
        first_vector,
        first_square,
        second_inner,
        second_outer,
        second_mix,
        readout_first.reshape(1, 128),
        readout_second.reshape(1, 128),
    )
    energy, up, mid, down = pair_program(layer, low, high, weights)
    folded = mid + lax.ppermute(up, "gz", ring("gz", 1)) + lax.ppermute(down, "gz", ring("gz", -1))
    total = folded[1] + lax.ppermute(folded[2], "gy", ring("gy", 1))
    total = total + lax.ppermute(folded[0], "gy", ring("gy", -1))
    return (energy.reshape(64), -total[0:3, 0:64])


def solution(mesh):
    spread = ("gx", "gy", "gz")
    placed = (P(None, spread), P(spread), P(spread, None), P(spread)) + (P(),) * 11
    return jax.shard_map(
        shards,
        mesh=mesh,
        in_specs=placed,
        out_specs=(P(spread), P(None, spread)),
        check_vma=False,
    )
```

```python
import functools

import jax
import jax.numpy as jnp
from jax import lax
from jax.experimental import pallas as pl
from jax.experimental.pallas import tpu as pltpu
from jax.sharding import PartitionSpec as P

F32 = jnp.float32
BF16 = jnp.bfloat16
I32 = jnp.int32
TILE = 256
MAX_TILES = 132
WINDOW = 64
UNROLL = 3
SCATTER = 6
KEPT_TILES = 30
KEPT_CORE_TILES = 8
INTERPRET = False

COLUMNS = [
    (1 + ((col >> 3) * 2 + ((col >> 1) & 1) + 1) % 4, 1 + (((col >> 2) & 1) * 2 + (col & 1) + 1) % 4)
    for col in range(16)
]
LIST_BASE = {1: 0, 2: 6, 3: 8, 4: 16}
LIST_STEP = {1: 3, 2: 5, 3: 5, 4: 3}
COORD_BASE = {-1: 2, 0: 10, 1: 18}
COORD_STEP = {-1: 3, 0: 5, 1: 3}


def split(x):
    high = x.astype(BF16)
    return high, (x - high.astype(F32)).astype(BF16)


def three(x, axis):
    high, low = split(x)
    return jnp.concatenate([high, low, high], axis=axis)


def three_weights(w, axis):
    high, low = split(w)
    return jnp.concatenate([high, high, low], axis=axis)


def dot(a, b):
    return lax.dot_general(a, b, (((1,), (0,)), ((), ())), preferred_element_type=F32)


def dot_t(a, b):
    return lax.dot_general(a, b, (((1,), (1,)), ((), ())), preferred_element_type=F32)


def lanes_of(table, index):
    return jnp.take_along_axis(table, index, axis=1, mode="promise_in_bounds")


def silu_pair(x):
    gate = 1.0 / (1.0 + jnp.exp(-x))
    value = x * gate
    return value, gate + value * (1.0 - gate)


def pack_kernel(pos_ref, species_ref, counts_ref, neighbors_ref, out_ref):
    ids = neighbors_ref[...].astype(F32)
    joined = jnp.concatenate([ids[:32], ids[32:]], axis=1)
    for part in range(4):
        out_ref[part] = joined[part * 8 : part * 8 + 8]
    rows = jnp.concatenate(
        [
            pos_ref[...],
            species_ref[...].astype(F32),
            counts_ref[...].astype(F32),
            jnp.zeros((3, 64), F32),
        ],
        axis=0,
    )
    out_ref[4] = jnp.concatenate([rows, rows], axis=1)


def iota(shape, axis):
    return lax.broadcasted_iota(I32, shape, axis)


def main_kernel(
    own_ref,
    low_ref,
    high_ref,
    emb_ref,
    fi_ref,
    fo_ref,
    fs_ref,
    fv_ref,
    fq_ref,
    si_ref,
    so_ref,
    sm_ref,
    rf_ref,
    rs_ref,
    energy_ref,
    up_ref,
    mid_ref,
    down_ref,
    table,
    mask_buf,
    lists,
    raw,
    counted_buf,
    rowbuf,
    buf,
    bes_buf,
    dbes_buf,
    pair_buf,
    offs_vmem,
    offs,
    last_row,
    sem,
    acc,
    vec_t,
    slope_t,
    feat_t,
    feat_grad,
    w_acc,
    grad_lhs,
    expand,
    saved,
    saved_core,
    saved_pair_grad,
    box_acc,
    emb_pad,
):
    lane8 = iota((8, 128), 1)
    sub8 = iota((8, 128), 0)
    upper = lane8 >= 64
    layer_refs = {-1: low_ref, 0: own_ref, 1: high_ref}

    for dy in (-1, 0, 1):
        for dz in (-1, 0, 1):
            ref = layer_refs[dz]
            base = COORD_BASE[dy]
            joined = jnp.where(upper, ref[base + COORD_STEP[dy]], ref[base])
            shift_x = jnp.where(upper, 12.0, 0.0)
            shift = jnp.where(
                sub8 == 0, shift_x, jnp.where(sub8 == 1, 12.0 * dy, jnp.where(sub8 == 2, 12.0 * dz, 0.0))
            )
            joined = joined + shift
            row = (dy + 1) * 3 + dz + 1
            for comp in range(5):
                table[comp, row] = jnp.broadcast_to(joined[comp : comp + 1], (8, 128))

    for col, (y, z) in enumerate(COLUMNS):
        layer = layer_refs[(z >> 1) - 1]
        for xd in range(2):
            lists[col * 2 + xd] = layer[LIST_BASE[y] + xd * LIST_STEP[y] + (z & 1)]

    def place_of(part):
        col, xd = part >> 1, part & 1
        y = 1 + (((col >> 3) * 2 + ((col >> 1) & 1) + 1) & 3)
        z = 1 + ((((col >> 2) & 1) * 2 + (col & 1) + 1) & 3)
        lane = xd * 64 + (y & 1) * 16 + (z & 1) * 8
        return y, z, xd, (y >> 1) * 3 + (z >> 1), lane

    def distances(part, carry):
        y, z, xd, row_l, base_l = place_of(part)
        y_low = jnp.where(y >= 3, 1, 0)
        z_low = jnp.where(z >= 3, 1, 0)
        row0 = y_low * 3 + z_low
        tile = lists[part].astype(I32)
        r1 = ((tile >> 3) & 3) + 1
        q1 = ((tile >> 5) & 3) + 1
        p1 = ((tile >> 7) & 3) + 1
        x_side = (1 - ((p1 >> 1) & 1)) ^ xd
        y_index = (q1 >> 1) + ((y >> 1) - 1 - y_low)
        z_index = (r1 >> 1) + ((z >> 1) - 1 - z_low)
        lane = x_side * 64 + (p1 & 1) * 32 + (q1 & 1) * 16 + (r1 & 1) * 8 + (tile & 7)
        lane_l = jnp.where(upper, 32, 0) + sub8 + base_l
        y_zero = y_index == 0
        z_zero = z_index == 0

        def fetch(comp):
            low = jnp.where(
                z_zero, lanes_of(table[comp, row0], lane), lanes_of(table[comp, row0 + 1], lane)
            )
            top = jnp.where(
                z_zero, lanes_of(table[comp, row0 + 3], lane), lanes_of(table[comp, row0 + 4], lane)
            )
            return jnp.where(y_zero, low, top)

        d = [fetch(comp) - lanes_of(table[comp, row_l], lane_l) for comp in range(3)]
        d[0] = jnp.where(d[0] > 12.0, d[0] - 24.0, jnp.where(d[0] < -12.0, d[0] + 24.0, d[0]))
        species = fetch(3)
        count = lanes_of(table[4, row_l], lane_l)
        square = d[0] * d[0] + d[1] * d[1] + d[2] * d[2] + 0.25
        slot = (lane8 & 63).astype(F32)
        reach = (square < 36.0) & (slot < count)
        inside = ((y_index >> 1) == 0) & ((z_index >> 1) == 0)
        live = jnp.where(reach & inside, 1.0, 0.0)
        code = (row0 + y_index * 3 + z_index) * 128 + lane
        rows = pl.ds(pl.multiple_of(part * 8, 8), 8)
        mask_buf[rows, :] = live
        raw[0, rows, :] = d[0]
        raw[1, rows, :] = d[1]
        raw[2, rows, :] = d[2]
        raw[3, rows, :] = species
        raw[4, rows, :] = code.astype(F32)
        return carry

    lax.fori_loop(0, 32, distances, 0, unroll=4)

    mask = mask_buf[...].astype(BF16)
    upto = jnp.where(iota((128, 128), 0) <= iota((128, 128), 1), 1.0, 0.0).astype(BF16)
    within = dot(mask, upto)
    totals = dot_t(jnp.ones((8, 128), BF16), mask)
    before = jnp.where(iota((256, 256), 0) < iota((256, 256), 1), 1.0, 0.0).astype(BF16)
    starts = dot(totals.astype(BF16), before)
    offs_vmem[:, 0:256] = starts.astype(I32)
    offs_vmem[:, 256:512] = totals.astype(I32)
    copy = pltpu.make_async_copy(offs_vmem, offs, sem)
    copy.start()

    counted_buf[...] = within

    def to_front(part, carry):
        _, _, _, row_l, base_l = place_of(part)
        at = pl.multiple_of(part * 8, 8)
        rows = pl.ds(at, 8)
        counted = counted_buf[rows, :]
        wanted = (lane8 + 1).astype(F32)
        place = jnp.zeros((8, 128), I32)
        for step in (64, 32, 16, 8, 4, 2, 1):
            probe = lanes_of(counted, place + (step - 1))
            place = jnp.where(probe < wanted, place + step, place)
        half = jnp.where(place >= 64, 1, 0)
        atom = (at + sub8) * 2 + half
        code_l = row_l * 128 + base_l + sub8 + half * 32
        fields = [lanes_of(raw[k, rows, :], place) for k in range(5)]
        fields += [atom.astype(F32), code_l.astype(F32)]
        for k, field in enumerate(fields):
            rowbuf[pl.ds(at * 8 + k, 8, stride=8), :] = field
        return carry

    lax.fori_loop(0, 32, to_front, 0, unroll=16)

    copy.wait()

    def join_row(r, current):
        start = offs[0, r]
        length = offs[0, 256 + r]
        shift = start & 127
        rolled = pltpu.roll(rowbuf[pl.ds(r * 8, 8), :], shift, 1)
        current = jnp.where(lane8 >= shift, rolled, current)
        buf[pl.ds((start >> 7) * 8, 8), :] = current
        last_row[start >> 8] = r
        return jnp.where(shift + length >= 128, rolled, current)

    current = lax.fori_loop(0, 256, join_row, jnp.zeros((8, 128), F32), unroll=16)
    total = offs[0, 255] + offs[0, 511]
    core_total = offs[0, 64]
    buf[pl.ds((total >> 7) * 8, 8), :] = current
    last_row[jnp.maximum(total - 1, 0) >> 8] = 255
    tiles = (total + (TILE - 1)) // TILE
    core_tiles = (core_total + (TILE - 1)) // TILE
    steps = (tiles + UNROLL - 1) // UNROLL
    scatters = (tiles + SCATTER - 1) // SCATTER

    def basis(chunk, carry):
        at = chunk * 64
        field = [buf[pl.ds(at + k, 8, stride=8), :] for k in range(7)]
        valid = (chunk * 1024 + sub8 * 128 + lane8) < total
        d = [jnp.where(valid, field[k], 100.0) for k in range(3)]
        species = jnp.where(valid, field[3], 0.0)
        code = jnp.where(valid, field[4], 0.0).astype(I32)
        atom = jnp.where(valid, field[5], -1.0)
        code_l = jnp.where(valid, field[6], 0.0)
        square = d[0] * d[0] + d[1] * d[1] + d[2] * d[2] + 0.25
        rho = jnp.sqrt(square)
        inv = 1.0 / rho
        t = jnp.where(rho < 6.0, rho * (1.0 / 6.0), 1.0)
        inside = valid & (rho < 6.0)
        angle = t * 3.14159265358979 - 1.5707963267948966
        a2 = angle * angle
        sin_a = angle * (
            1.0
            + a2
            * (
                -1.0 / 6
                + a2
                * (
                    1.0 / 120
                    + a2 * (-1.0 / 5040 + a2 * (1.0 / 362880 + a2 * (-1.0 / 39916800 + a2 / 6227020800.0)))
                )
            )
        )
        cos_a = 1.0 + a2 * (
            -0.5
            + a2
            * (
                1.0 / 24
                + a2
                * (
                    -1.0 / 720
                    + a2
                    * (1.0 / 40320 + a2 * (-1.0 / 3628800 + a2 * (1.0 / 479001600 - a2 / 87178291200.0)))
                )
            )
        )
        sine, cosine = cos_a, -sin_a
        t2 = t * t
        t5 = t2 * t2 * t
        f = 1.0 + t5 * t * (-28.0 + t * (48.0 - 21.0 * t))
        f = jnp.where(inside, f, 0.0)
        one = 1.0 - t
        df = jnp.where(inside, -28.0 * t5 * one * one, 0.0)
        scale = 0.5773502691896258
        amount = scale * inv * f
        slope = scale * inv * (df - inv * f)
        s_prev, c_prev = jnp.zeros((8, 128), F32), jnp.ones((8, 128), F32)
        s_now, c_now = sine, cosine
        for n in range(8):
            bes_buf[pl.ds(at + n, 8, stride=8), :] = s_now * amount
            dbes_buf[pl.ds(at + n, 8, stride=8), :] = (
                c_now * amount * ((n + 1) * 0.5235987755982988) + s_now * slope
            )
            s_now, s_prev = 2.0 * cosine * s_now - s_prev, s_now
            c_now, c_prev = 2.0 * cosine * c_now - c_prev, c_now
        row = code >> 7
        lane = code & 127
        row_y = jnp.where(row >= 6, 2, jnp.where(row >= 3, 1, 0))
        row_z = row - 3 * row_y
        y = row_y * 2 + ((lane >> 4) & 1) - 1
        z = row_z * 2 + ((lane >> 3) & 1) - 1
        near = (y >= 0) & (y < 4) & (z >= 0) & (z < 4)
        y = (y + 3) & 3
        z = (z + 3) & 3
        column = (y >> 1) * 8 + (z >> 1) * 4 + (y & 1) * 2 + (z & 1)
        source = column * 32 + ((lane >> 6) & 1) * 16 + (lane & 7) * 2 + ((lane >> 5) & 1)
        source = jnp.where(near, source, -1)
        both = code.astype(F32) * 2048.0 + code_l
        kept = [d[0] * inv, d[1] * inv, d[2] * inv, inv, species, source.astype(F32), atom, both]
        for k, value in enumerate(kept):
            pair_buf[pl.ds(at + k, 8, stride=8), :] = value
        return carry

    lax.fori_loop(0, (scatters * SCATTER * TILE + 1023) // 1024, basis, 0)

    fi3 = jnp.concatenate([fi_ref[...], jnp.zeros((24, 64), F32)], axis=0)
    si3 = jnp.concatenate([si_ref[...], jnp.zeros((24, 64), F32)], axis=0)

    def inner_weights(padded):
        w = padded.T[:, 0:8]
        high = w.astype(BF16).astype(F32)
        low = w - high
        return jnp.concatenate([high, high, low, jnp.zeros((64, 8), F32)], axis=1).astype(BF16)

    fi_t3 = inner_weights(fi3)
    si_t3 = inner_weights(si3)
    fo_t3 = three_weights(fo_ref[...].T, 1)
    so_t3 = three_weights(so_ref[...].T, 1)
    emb_pad[...] = jnp.zeros((128, 128), F32)
    emb_pad[0:89, :] = emb_ref[...]
    emb_t2 = jnp.concatenate(split(emb_pad[...].T), axis=1)

    def tile_rows(ref, t):
        at = t * 16
        return jnp.concatenate([ref[pl.ds(at, 8), :], ref[pl.ds(at + 8, 8), :]], axis=1)

    def stacked(ref, t):
        rows = tile_rows(ref, t)
        high = rows.astype(BF16).astype(F32)
        stack = jnp.concatenate([high, rows - high, high, jnp.zeros((8, TILE), F32)], axis=0)
        return stack.astype(BF16)

    def radial_of(t, inner, outer):
        hidden, slope = silu_pair(dot(inner, stacked(bes_buf, t)))
        rate = dot(inner, stacked(dbes_buf, t)) * slope
        return dot(outer, three(hidden, 0)), dot(outer, three(rate, 0))

    def onehot(index_row, rows):
        hit = iota((rows, index_row.shape[1]), 0) == index_row.astype(I32)
        return jnp.where(hit, 1.0, 0.0).astype(BF16)

    def sender_of(species_row):
        hot = onehot(species_row, 128)
        return dot(emb_t2, jnp.concatenate([hot, hot], axis=0))

    def first_of(t):
        before = jnp.clip(t - 1, 0, jnp.maximum(tiles - 1, 0))
        return jnp.where(t == 0, 0, last_row[before]) * 2

    acc[...] = jnp.zeros(acc.shape, F32)

    def first_terms(t):
        weights, rates = radial_of(t, fi_t3, fo_t3)
        pair = tile_rows(pair_buf, t)
        sender = sender_of(pair[4:5])
        message = weights[0:128] * sender
        rg = weights[128:256] * sender
        return pair, message, rg, rates[0:128] * sender, rates[128:256] * sender

    def layer_one(step, carry):
        done = []
        for part in range(UNROLL):
            t = step * UNROLL + part
            pair, message, rg, rate_0, rate_1 = first_terms(t)
            kept = jnp.minimum(t, KEPT_TILES)
            saved[kept, 0:128, :] = rg
            saved[kept, 128:256, :] = rate_0
            saved[kept, 256:384, :] = rate_1
            saved_pair_grad[t] = jnp.zeros((8, TILE), F32)
            both = jnp.concatenate(split(message), axis=0), jnp.concatenate(split(rg), axis=0)
            done.append((t, first_of(t) & -8, pair, both))

        def window(entry, w):
            _, base, pair, (m_parts, v_parts) = entry
            at = base + w * WINDOW
            unit = [split(pair[k : k + 1]) for k in range(3)]
            hot = onehot(pair[6:7] - at.astype(F32), WINDOW)
            u_high = jnp.concatenate([hot * high for high, _ in unit], axis=0)
            u_low = jnp.concatenate([hot * low for _, low in unit], axis=0)
            m = dot_t(hot, m_parts)
            v = dot_t(u_high, v_parts)
            m = m[:, 0:128] + m[:, 128:256]
            v = v[:, 0:128] + v[:, 128:256] + dot_t(u_low, v_parts[0:128])
            return pl.ds(pl.multiple_of(at, 8), WINDOW), m, v

        def add(rows, m, v):
            acc[0, rows, :] += m
            for x in range(3):
                acc[1 + x, rows, :] += v[x * WINDOW : (x + 1) * WINDOW]

        for sums in [window(entry, 0) for entry in done]:
            add(*sums)
        counts = [
            jnp.where(t < tiles, (last_row[t] * 2 + 1 - base) // WINDOW + 1, 1)
            for t, base, _, _ in done
        ]
        most = counts[0]
        for count in counts[1:]:
            most = jnp.maximum(most, count)

        @pl.when(most > 1)
        def _():
            for count, entry in zip(counts, done):

                def more(w, carry, entry=entry):
                    add(*window(entry, w))
                    return carry

                lax.fori_loop(1, count, more, 0)

        return carry

    lax.fori_loop(0, steps, layer_one, 0)

    parts = []
    for group in range(4):
        merged = None
        for sub in range(4):
            col = group * 4 + sub
            y, z = COLUMNS[col]
            row, b, c = (y >> 1) * 3 + (z >> 1), y & 1, z & 1
            local = lane8 & 31
            index = ((local >> 4) & 1) * 64 + (local & 1) * 32 + ((local >> 1) & 7) + b * 16 + c * 8
            got = lanes_of(table[3, row], index)
            merged = got if merged is None else jnp.where((lane8 >> 5) == sub, got, merged)
        parts.append(merged)
    species_row = jnp.concatenate(parts, axis=1)[0:1]
    node_t = sender_of(species_row)
    fv_t3 = three_weights(fv_ref[...].T, 1)
    square_t = jnp.zeros((128, 512), F32)
    for x in range(3):
        v3 = three(acc[1 + x, 0:512, :] * 0.25, 1)
        value = dot_t(fv_t3, v3)
        vec_t[x] = value
        square_t = square_t + value * value
        high, low = split(value)
        feat_t[0, 128 + x * 128 : 256 + x * 128, :] = high
        feat_t[1, 128 + x * 128 : 256 + x * 128, :] = low
    fs_t3 = three_weights(fs_ref[...].T, 1)
    fq_t3 = three_weights(fq_ref[...].T, 1)
    pre = dot_t(fs_t3, three(acc[0, 0:512, :] * 0.25, 1))
    pre = pre + dot(fs_t3, three(node_t, 0)) + dot(fq_t3, three(square_t, 0))
    scal_t, slope = silu_pair(pre)
    slope_t[...] = slope
    high, low = split(scal_t)
    feat_t[0, 0:128, :] = high
    feat_t[1, 0:128, :] = low
    scal_core = scal_t[:, 0:128]

    w_acc[...] = jnp.zeros((128, 128), F32)

    def second_terms(t):
        weights, rates = radial_of(t, si_t3, so_t3)
        pair = tile_rows(pair_buf, t)
        hot = onehot(pair[5:6], 512)
        feat = dot(feat_t[...].reshape(1024, 512), hot)
        feat = feat[0:512] + feat[512:1024]
        proj = pair[0:1] * feat[128:256] + pair[1:2] * feat[256:384] + pair[2:3] * feat[384:512]
        rate = rates[0:128] * feat[0:128] + rates[128:256] * proj
        message = weights[0:128] * feat[0:128] + weights[128:256] * proj
        return pair, message, feat[128:512], weights, rate

    def layer_two(t, carry):
        pair, message, vectors, weights, rate = second_terms(t)
        kept = jnp.minimum(t, KEPT_CORE_TILES)
        saved_core[kept, 0:384, :] = vectors
        saved_core[kept, 384:640, :] = weights
        saved_core[kept, 640:768, :] = rate
        high, low = split(message)
        member = onehot(pair[6:7], 128)
        w_acc[...] += dot_t(high, member) + dot_t(low, member)
        return carry

    lax.fori_loop(0, core_tiles, layer_two, 0)

    mixed = w_acc[...] * 0.25 + scal_core
    rs_col = jnp.broadcast_to(rs_ref[...], (128, 128)).T
    rf_col = jnp.broadcast_to(rf_ref[...], (128, 128)).T
    out, out_slope = silu_pair(dot(three_weights(sm_ref[...].T, 1), three(mixed, 0)))
    energy = jnp.sum(out * rs_col + scal_core * rf_col, axis=0, keepdims=True)
    index = (((lane8 >> 3) & 3) * 16 + (lane8 & 7)) * 2 + ((lane8 >> 5) & 1)
    index = jnp.where(lane8 < 64, ((lane8 >> 3) & 3) * 32 + (lane8 & 7) * 2 + ((lane8 >> 5) & 1), 0)
    energy_ref[...] = lanes_of(jnp.broadcast_to(energy, (8, 128)), index)[0:1, 0:64]

    mixed_grad = dot(three_weights(sm_ref[...], 1), three(rs_col * out_slope, 0))
    w_grad2 = jnp.concatenate(split(mixed_grad * 0.25), axis=1)
    feat_grad[...] = jnp.zeros((512, 512), F32)
    feat_grad[0:128, 0:128] = mixed_grad + rf_col

    def layer_two_back(t, carry, again):
        pair = tile_rows(pair_buf, t)
        member = onehot(pair[6:7], 128)
        w_grad = dot(w_grad2, jnp.concatenate([member, member], axis=0))
        if again:
            _, _, vectors, weights, rate = second_terms(t)
        else:
            vectors, weights = saved_core[t, 0:384, :], saved_core[t, 384:640, :]
            rate = saved_core[t, 640:768, :]
        proj_grad = w_grad * weights[128:256]
        grads = [jnp.sum(w_grad * rate, axis=0, keepdims=True)]
        sends = [w_grad * weights[0:128]]
        for x in range(3):
            part = vectors[x * 128 : 128 + x * 128]
            grads.append(jnp.sum(proj_grad * part, axis=0, keepdims=True))
            sends.append(proj_grad * pair[x : x + 1])
        saved_pair_grad[t] = jnp.concatenate(grads + [jnp.zeros((4, TILE), F32)], axis=0)
        high, low = split(jnp.concatenate(sends, axis=0))
        hot = onehot(pair[5:6], 512)
        feat_grad[...] += dot_t(high, hot) + dot_t(low, hot)
        return carry

    kept_core = jnp.minimum(core_tiles, KEPT_CORE_TILES)
    lax.fori_loop(0, kept_core, functools.partial(layer_two_back, again=False), 0)
    lax.fori_loop(kept_core, core_tiles, functools.partial(layer_two_back, again=True), 0)

    pre_grad3 = three(feat_grad[0:128, :] * slope_t[...], 0)
    m_grad = dot(three_weights(fs_ref[...], 1), pre_grad3)
    square_grad = dot(three_weights(fq_ref[...], 1), pre_grad3)
    fv_b3 = three_weights(fv_ref[...], 1)
    message_grads = [m_grad]
    for x in range(3):
        part = feat_grad[128 + x * 128 : 256 + x * 128, :] + 2.0 * vec_t[x] * square_grad
        message_grads.append(dot(fv_b3, three(part, 0)))
    for kind in range(4):
        wide = jnp.concatenate([message_grads[kind] * 0.25, jnp.zeros((128, 128), F32)], axis=1)
        for odd, part in enumerate((wide, pltpu.roll(wide, 576, 1))):
            high, low = split(part)
            for w in range(4):
                rows = pl.ds(kind * 128, 128)
                grad_lhs[2 * w + odd, rows, 0:128] = high[:, w * 128 : (w + 1) * 128]
                grad_lhs[2 * w + odd, rows, 128:256] = low[:, w * 128 : (w + 1) * 128]

    box_acc[...] = jnp.zeros((96, 128), F32)

    def expanded(pair, w):
        member = onehot(pair[6:7] - (w * 64).astype(F32), 128)
        return dot(grad_lhs[w], jnp.concatenate([member, member], axis=0))

    def back_tiles(step, again, many):
        for part in range(UNROLL):
            t = step * UNROLL + part
            pair = tile_rows(pair_buf, t)
            first = first_of(t) >> 6
            moved = expanded(pair, first)
            if many:
                expand[...] = moved
                last = jnp.where(t < tiles, (last_row[t] * 2 + 1) >> 6, 0)

                def more(w, carry, pair=pair, first=first):
                    expand[...] += expanded(pair, first + 2 * w)
                    return carry

                lax.fori_loop(1, ((last - first) >> 1) + 1, more, 0)
                moved = expand[...]
            if again:
                _, _, rg, rate_0, rate_1 = first_terms(t)
            else:
                rg, rate_0, rate_1 = (saved[t, k * 128 : k * 128 + 128, :] for k in range(3))
            earlier = saved_pair_grad[t]
            rho_grad = earlier[0:1] + jnp.sum(moved[0:128] * rate_0, axis=0, keepdims=True)
            unit_grad = []
            for x in range(3):
                v_grad = moved[128 + x * 128 : 256 + x * 128]
                along = jnp.sum(v_grad * rate_1, axis=0, keepdims=True)
                rho_grad = rho_grad + pair[x : x + 1] * along
                across = jnp.sum(v_grad * rg, axis=0, keepdims=True)
                unit_grad.append(across + earlier[1 + x : 2 + x])
            unit = [pair[x : x + 1] for x in range(3)]
            inner = unit[0] * unit_grad[0] + unit[1] * unit_grad[1] + unit[2] * unit_grad[2]
            inv = pair[3:4]
            values = []
            for x in range(3):
                values.append((unit_grad[x] - unit[x] * inner) * inv + rho_grad * unit[x])
            for x in range(3):
                saved_pair_grad[t, x : x + 1, :] = values[x]

    def layer_one_back(step, carry):
        crossing = False
        for part in range(UNROLL):
            t = step * UNROLL + part
            last = jnp.where(t < tiles, (last_row[t] * 2 + 1) >> 6, 0)
            crossing = crossing | (last > (first_of(t) >> 6) + 1)

        @pl.when(crossing)
        def _():
            back_tiles(step, False, True)

        @pl.when(jnp.logical_not(crossing))
        def _():
            back_tiles(step, False, False)

        return carry

    def layer_one_again(step, carry):
        back_tiles(step, True, True)
        return carry

    kept_steps = jnp.minimum(steps, KEPT_TILES // UNROLL)
    lax.fori_loop(0, kept_steps, layer_one_back, 0)
    lax.fori_loop(kept_steps, steps, layer_one_again, 0)

    def scatter(group, carry):
        total_grad = None
        for part in range(SCATTER):
            t = group * SCATTER + part
            pair = tile_rows(pair_buf, t)
            values = []
            for x in range(3):
                value = jnp.where(pair[6:7] >= 0.0, saved_pair_grad[t, x : x + 1, :], 0.0)
                high = value.astype(BF16).astype(F32)
                values += [high, value - high]
            both = pair[7:8].astype(I32)
            rows, lanes = [], []
            for code, sign in ((both >> 11, 1.0), (both & 2047, -1.0)):
                row = jnp.broadcast_to(code >> 7, (16, TILE)) == iota((16, TILE), 0)
                stack = [jnp.where(row, sign * value, 0.0) for value in values]
                rows.append(jnp.concatenate(stack, axis=0).astype(BF16))
                lanes.append(onehot(code & 127, 128))
            moved = dot_t(jnp.concatenate(rows, axis=1), jnp.concatenate(lanes, axis=1))
            total_grad = moved if total_grad is None else total_grad + moved
        box_acc[...] += total_grad
        return carry

    lax.fori_loop(0, scatters, scatter, 0)

    for comp in range(3):
        grid = box_acc[comp * 32 : comp * 32 + 16, :] + box_acc[comp * 32 + 16 : comp * 32 + 32, :]
        for dz, ref in ((-1, down_ref), (0, mid_ref), (1, up_ref)):
            for dy in range(3):
                row = dy * 3 + dz + 1
                ref[dy, comp : comp + 1, :] = grid[row : row + 1, :]
    for ref in (down_ref, mid_ref, up_ref):
        for dy in range(3):
            ref[dy, 3:8, :] = jnp.zeros((5, 128), F32)


def pair_program(own, low, high, weights):
    vm = pltpu.VMEM
    pair_rows = (MAX_TILES * 2 + 6) * 8
    scratch = [
        vm((5, 9, 8, 128), F32),
        vm((256, 128), F32),
        vm((32, 8, 128), F32),
        vm((5, 256, 128), F32),
        vm((256, 128), F32),
        vm((2048, 128), F32),
        vm((pair_rows, 128), F32),
        vm((pair_rows, 128), F32),
        vm((pair_rows, 128), F32),
        vm((pair_rows, 128), F32),
        vm((8, 512), I32),
        pltpu.SMEM((8, 512), I32),
        pltpu.SMEM((256,), I32),
        pltpu.SemaphoreType.DMA,
        vm((4, 512 + WINDOW, 128), F32),
        vm((3, 128, 512), F32),
        vm((128, 512), F32),
        vm((2, 512, 512), BF16),
        vm((512, 512), F32),
        vm((128, 128), F32),
        vm((8, 512, 256), BF16),
        vm((512, TILE), F32),
        vm((KEPT_TILES + 1, 384, TILE), F32),
        vm((KEPT_CORE_TILES + 1, 768, TILE), F32),
        vm((MAX_TILES, 8, TILE), F32),
        vm((96, 128), F32),
        vm((128, 128), F32),
    ]
    whole = pl.BlockSpec(memory_space=pltpu.VMEM)
    piece = jax.ShapeDtypeStruct((3, 8, 128), F32)
    return pl.pallas_call(
        main_kernel,
        out_shape=(jax.ShapeDtypeStruct((1, 64), F32), piece, piece, piece),
        in_specs=[whole] * (3 + len(weights)),
        out_specs=(whole,) * 4,
        scratch_shapes=scratch,
        compiler_params=pltpu.CompilerParams(vmem_limit_bytes=42 * 1024 * 1024),
        interpret=INTERPRET,
    )(own, low, high, *weights)


def pack(positions, species, counts, neighbors):
    whole = pl.BlockSpec(memory_space=pltpu.VMEM)
    return pl.pallas_call(
        pack_kernel,
        out_shape=jax.ShapeDtypeStruct((5, 8, 128), F32),
        in_specs=[whole] * 4,
        out_specs=whole,
        interpret=INTERPRET,
    )(positions, species.reshape(1, 64), counts.reshape(1, 64), neighbors)


def join_y(own, below, above):
    return jnp.concatenate(
        [below[2:5], below[7:10], own, above[0:2], above[4:7], above[9:10]], axis=0
    )


def ring(axis, step):
    count = lax.axis_size(axis)
    return [(i, (i + step) % count) for i in range(count)]


def shards(
    positions,
    species,
    neighbors,
    neighbor_counts,
    embedding,
    first_inner,
    first_outer,
    first_scalar,
    first_vector,
    first_square,
    second_inner,
    second_outer,
    second_mix,
    readout_first,
    readout_second,
):
    packed = pack(positions, species, neighbor_counts, neighbors)
    partner = lax.ppermute(packed, "gx", ring("gx", 1))
    both = jnp.concatenate([packed, partner], axis=0)
    below = lax.ppermute(both, "gy", ring("gy", 1))
    above = lax.ppermute(both, "gy", ring("gy", -1))
    layer = join_y(both, below, above)
    low = lax.ppermute(layer, "gz", ring("gz", 1))
    high = lax.ppermute(layer, "gz", ring("gz", -1))
    weights = (
        embedding,
        first_inner,
        first_outer,
        first_scalar,
        first_vector,
        first_square,
        second_inner,
        second_outer,
        second_mix,
        readout_first.reshape(1, 128),
        readout_second.reshape(1, 128),
    )
    energy, up, mid, down = pair_program(layer, low, high, weights)
    folded = mid + lax.ppermute(up, "gz", ring("gz", 1)) + lax.ppermute(down, "gz", ring("gz", -1))
    total = folded[1] + lax.ppermute(folded[2], "gy", ring("gy", 1))
    total = total + lax.ppermute(folded[0], "gy", ring("gy", -1))
    return (energy.reshape(64), -total[0:3, 0:64])


def solution(mesh):
    spread = ("gx", "gy", "gz")
    placed = (P(None, spread), P(spread), P(spread, None), P(spread)) + (P(),) * 11
    return jax.shard_map(
        shards,
        mesh=mesh,
        in_specs=placed,
        out_specs=(P(spread), P(None, spread)),
        check_vma=False,
    )
```

```python
import functools

import jax
import jax.numpy as jnp
from jax import lax
from jax.experimental import pallas as pl
from jax.experimental.pallas import tpu as pltpu
from jax.sharding import PartitionSpec as P

F32 = jnp.float32
BF16 = jnp.bfloat16
I32 = jnp.int32
TILE = 256
MAX_TILES = 132
WINDOW = 64
UNROLL = 3
SCATTER = 6
KEPT_TILES = 30
KEPT_CORE_TILES = 8
INTERPRET = False

COLUMNS = [
    (1 + ((col >> 3) * 2 + ((col >> 1) & 1) + 1) % 4, 1 + (((col >> 2) & 1) * 2 + (col & 1) + 1) % 4)
    for col in range(16)
]
LIST_BASE = {1: 0, 2: 6, 3: 8, 4: 16}
LIST_STEP = {1: 3, 2: 5, 3: 5, 4: 3}
COORD_BASE = {-1: 2, 0: 10, 1: 18}
COORD_STEP = {-1: 3, 0: 5, 1: 3}


def split(x):
    high = x.astype(BF16)
    return high, (x - high.astype(F32)).astype(BF16)


def three(x, axis):
    high, low = split(x)
    return jnp.concatenate([high, low, high], axis=axis)


def three_weights(w, axis):
    high, low = split(w)
    return jnp.concatenate([high, high, low], axis=axis)


def dot(a, b):
    return lax.dot_general(a, b, (((1,), (0,)), ((), ())), preferred_element_type=F32)


def dot_t(a, b):
    return lax.dot_general(a, b, (((1,), (1,)), ((), ())), preferred_element_type=F32)


def lanes_of(table, index):
    return jnp.take_along_axis(table, index, axis=1, mode="promise_in_bounds")


def silu_pair(x):
    gate = 1.0 / (1.0 + jnp.exp(-x))
    value = x * gate
    return value, gate + value * (1.0 - gate)


def pack_kernel(pos_ref, species_ref, counts_ref, neighbors_ref, out_ref):
    ids = neighbors_ref[...].astype(F32)
    joined = jnp.concatenate([ids[:32], ids[32:]], axis=1)
    for part in range(4):
        out_ref[part] = joined[part * 8 : part * 8 + 8]
    rows = jnp.concatenate(
        [
            pos_ref[...],
            species_ref[...].astype(F32),
            counts_ref[...].astype(F32),
            jnp.zeros((3, 64), F32),
        ],
        axis=0,
    )
    out_ref[4] = jnp.concatenate([rows, rows], axis=1)


def iota(shape, axis):
    return lax.broadcasted_iota(I32, shape, axis)


def main_kernel(
    own_ref,
    low_ref,
    high_ref,
    emb_hbm,
    fi_hbm,
    fo_hbm,
    fs_hbm,
    fv_hbm,
    fq_hbm,
    si_hbm,
    so_hbm,
    sm_hbm,
    rf_hbm,
    rs_hbm,
    energy_ref,
    up_ref,
    mid_ref,
    down_ref,
    table,
    mask_buf,
    lists,
    raw,
    counted_buf,
    rowbuf,
    buf,
    bes_buf,
    dbes_buf,
    pair_buf,
    offs_vmem,
    offs,
    last_row,
    sem,
    acc,
    vec_t,
    slope_t,
    feat_t,
    feat_grad,
    w_acc,
    grad_lhs,
    expand,
    saved,
    saved_core,
    saved_pair_grad,
    box_acc,
    emb_pad,
    emb_ref,
    fi_ref,
    fo_ref,
    fs_ref,
    fv_ref,
    fq_ref,
    si_ref,
    so_ref,
    sm_ref,
    rf_ref,
    rs_ref,
    weight_sem,
):
    sources = [emb_hbm, fi_hbm, fo_hbm, fs_hbm, fv_hbm, fq_hbm, si_hbm, so_hbm, sm_hbm, rf_hbm, rs_hbm]
    targets = [emb_ref, fi_ref, fo_ref, fs_ref, fv_ref, fq_ref, si_ref, so_ref, sm_ref, rf_ref, rs_ref]
    fetches = [
        pltpu.make_async_copy(source, target, weight_sem.at[k])
        for k, (source, target) in enumerate(zip(sources, targets))
    ]
    for fetch in fetches:
        fetch.start()
    lane8 = iota((8, 128), 1)
    sub8 = iota((8, 128), 0)
    upper = lane8 >= 64
    layer_refs = {-1: low_ref, 0: own_ref, 1: high_ref}

    for dy in (-1, 0, 1):
        for dz in (-1, 0, 1):
            ref = layer_refs[dz]
            base = COORD_BASE[dy]
            joined = jnp.where(upper, ref[base + COORD_STEP[dy]], ref[base])
            shift_x = jnp.where(upper, 12.0, 0.0)
            shift = jnp.where(
                sub8 == 0, shift_x, jnp.where(sub8 == 1, 12.0 * dy, jnp.where(sub8 == 2, 12.0 * dz, 0.0))
            )
            joined = joined + shift
            row = (dy + 1) * 3 + dz + 1
            for comp in range(5):
                table[comp, row] = jnp.broadcast_to(joined[comp : comp + 1], (8, 128))

    for col, (y, z) in enumerate(COLUMNS):
        layer = layer_refs[(z >> 1) - 1]
        for xd in range(2):
            lists[col * 2 + xd] = layer[LIST_BASE[y] + xd * LIST_STEP[y] + (z & 1)]

    def place_of(part):
        col, xd = part >> 1, part & 1
        y = 1 + (((col >> 3) * 2 + ((col >> 1) & 1) + 1) & 3)
        z = 1 + ((((col >> 2) & 1) * 2 + (col & 1) + 1) & 3)
        lane = xd * 64 + (y & 1) * 16 + (z & 1) * 8
        return y, z, xd, (y >> 1) * 3 + (z >> 1), lane

    def distances(part, carry):
        y, z, xd, row_l, base_l = place_of(part)
        y_low = jnp.where(y >= 3, 1, 0)
        z_low = jnp.where(z >= 3, 1, 0)
        row0 = y_low * 3 + z_low
        tile = lists[part].astype(I32)
        r1 = ((tile >> 3) & 3) + 1
        q1 = ((tile >> 5) & 3) + 1
        p1 = ((tile >> 7) & 3) + 1
        x_side = (1 - ((p1 >> 1) & 1)) ^ xd
        y_index = (q1 >> 1) + ((y >> 1) - 1 - y_low)
        z_index = (r1 >> 1) + ((z >> 1) - 1 - z_low)
        lane = x_side * 64 + (p1 & 1) * 32 + (q1 & 1) * 16 + (r1 & 1) * 8 + (tile & 7)
        lane_l = jnp.where(upper, 32, 0) + sub8 + base_l
        y_zero = y_index == 0
        z_zero = z_index == 0

        def pick(comp):
            low = jnp.where(
                z_zero, lanes_of(table[comp, row0], lane), lanes_of(table[comp, row0 + 1], lane)
            )
            top = jnp.where(
                z_zero, lanes_of(table[comp, row0 + 3], lane), lanes_of(table[comp, row0 + 4], lane)
            )
            return jnp.where(y_zero, low, top)

        d = [pick(comp) - lanes_of(table[comp, row_l], lane_l) for comp in range(3)]
        d[0] = jnp.where(d[0] > 12.0, d[0] - 24.0, jnp.where(d[0] < -12.0, d[0] + 24.0, d[0]))
        species = pick(3)
        count = lanes_of(table[4, row_l], lane_l)
        square = d[0] * d[0] + d[1] * d[1] + d[2] * d[2] + 0.25
        slot = (lane8 & 63).astype(F32)
        reach = (square < 36.0) & (slot < count)
        inside = ((y_index >> 1) == 0) & ((z_index >> 1) == 0)
        live = jnp.where(reach & inside, 1.0, 0.0)
        code = (row0 + y_index * 3 + z_index) * 128 + lane
        rows = pl.ds(pl.multiple_of(part * 8, 8), 8)
        mask_buf[rows, :] = live
        raw[0, rows, :] = d[0]
        raw[1, rows, :] = d[1]
        raw[2, rows, :] = d[2]
        raw[3, rows, :] = species
        raw[4, rows, :] = code.astype(F32)
        return carry

    lax.fori_loop(0, 32, distances, 0, unroll=4)

    mask = mask_buf[...].astype(BF16)
    upto = jnp.where(iota((128, 128), 0) <= iota((128, 128), 1), 1.0, 0.0).astype(BF16)
    within = dot(mask, upto)
    totals = dot_t(jnp.ones((8, 128), BF16), mask)
    before = jnp.where(iota((256, 256), 0) < iota((256, 256), 1), 1.0, 0.0).astype(BF16)
    starts = dot(totals.astype(BF16), before)
    offs_vmem[:, 0:256] = starts.astype(I32)
    offs_vmem[:, 256:512] = totals.astype(I32)
    copy = pltpu.make_async_copy(offs_vmem, offs, sem)
    copy.start()

    counted_buf[...] = within

    def to_front(part, carry):
        _, _, _, row_l, base_l = place_of(part)
        at = pl.multiple_of(part * 8, 8)
        rows = pl.ds(at, 8)
        counted = counted_buf[rows, :]
        wanted = (lane8 + 1).astype(F32)
        place = jnp.zeros((8, 128), I32)
        for step in (64, 32, 16, 8, 4, 2, 1):
            probe = lanes_of(counted, place + (step - 1))
            place = jnp.where(probe < wanted, place + step, place)
        half = jnp.where(place >= 64, 1, 0)
        atom = (at + sub8) * 2 + half
        code_l = row_l * 128 + base_l + sub8 + half * 32
        fields = [lanes_of(raw[k, rows, :], place) for k in range(5)]
        fields += [atom.astype(F32), code_l.astype(F32)]
        for k, field in enumerate(fields):
            rowbuf[pl.ds(at * 8 + k, 8, stride=8), :] = field
        return carry

    lax.fori_loop(0, 32, to_front, 0, unroll=16)

    copy.wait()

    def join_row(r, current):
        start = offs[0, r]
        length = offs[0, 256 + r]
        shift = start & 127
        rolled = pltpu.roll(rowbuf[pl.ds(r * 8, 8), :], shift, 1)
        current = jnp.where(lane8 >= shift, rolled, current)
        buf[pl.ds((start >> 7) * 8, 8), :] = current
        last_row[start >> 8] = r
        return jnp.where(shift + length >= 128, rolled, current)

    current = lax.fori_loop(0, 256, join_row, jnp.zeros((8, 128), F32), unroll=16)
    total = offs[0, 255] + offs[0, 511]
    core_total = offs[0, 64]
    buf[pl.ds((total >> 7) * 8, 8), :] = current
    last_row[jnp.maximum(total - 1, 0) >> 8] = 255
    tiles = (total + (TILE - 1)) // TILE
    core_tiles = (core_total + (TILE - 1)) // TILE
    steps = (tiles + UNROLL - 1) // UNROLL
    scatters = (tiles + SCATTER - 1) // SCATTER

    def basis(chunk, carry):
        at = chunk * 64
        field = [buf[pl.ds(at + k, 8, stride=8), :] for k in range(7)]
        valid = (chunk * 1024 + sub8 * 128 + lane8) < total
        d = [jnp.where(valid, field[k], 100.0) for k in range(3)]
        species = jnp.where(valid, field[3], 0.0)
        code = jnp.where(valid, field[4], 0.0).astype(I32)
        atom = jnp.where(valid, field[5], -1.0)
        code_l = jnp.where(valid, field[6], 0.0)
        square = d[0] * d[0] + d[1] * d[1] + d[2] * d[2] + 0.25
        rho = jnp.sqrt(square)
        inv = 1.0 / rho
        t = jnp.where(rho < 6.0, rho * (1.0 / 6.0), 1.0)
        inside = valid & (rho < 6.0)
        angle = t * 3.14159265358979 - 1.5707963267948966
        a2 = angle * angle
        sin_a = angle * (
            1.0
            + a2
            * (
                -1.0 / 6
                + a2
                * (
                    1.0 / 120
                    + a2 * (-1.0 / 5040 + a2 * (1.0 / 362880 + a2 * (-1.0 / 39916800 + a2 / 6227020800.0)))
                )
            )
        )
        cos_a = 1.0 + a2 * (
            -0.5
            + a2
            * (
                1.0 / 24
                + a2
                * (
                    -1.0 / 720
                    + a2
                    * (1.0 / 40320 + a2 * (-1.0 / 3628800 + a2 * (1.0 / 479001600 - a2 / 87178291200.0)))
                )
            )
        )
        sine, cosine = cos_a, -sin_a
        t2 = t * t
        t5 = t2 * t2 * t
        f = 1.0 + t5 * t * (-28.0 + t * (48.0 - 21.0 * t))
        f = jnp.where(inside, f, 0.0)
        one = 1.0 - t
        df = jnp.where(inside, -28.0 * t5 * one * one, 0.0)
        scale = 0.5773502691896258
        amount = scale * inv * f
        slope = scale * inv * (df - inv * f)
        s_prev, c_prev = jnp.zeros((8, 128), F32), jnp.ones((8, 128), F32)
        s_now, c_now = sine, cosine
        for n in range(8):
            bes_buf[pl.ds(at + n, 8, stride=8), :] = s_now * amount
            dbes_buf[pl.ds(at + n, 8, stride=8), :] = (
                c_now * amount * ((n + 1) * 0.5235987755982988) + s_now * slope
            )
            s_now, s_prev = 2.0 * cosine * s_now - s_prev, s_now
            c_now, c_prev = 2.0 * cosine * c_now - c_prev, c_now
        row = code >> 7
        lane = code & 127
        row_y = jnp.where(row >= 6, 2, jnp.where(row >= 3, 1, 0))
        row_z = row - 3 * row_y
        y = row_y * 2 + ((lane >> 4) & 1) - 1
        z = row_z * 2 + ((lane >> 3) & 1) - 1
        near = (y >= 0) & (y < 4) & (z >= 0) & (z < 4)
        y = (y + 3) & 3
        z = (z + 3) & 3
        column = (y >> 1) * 8 + (z >> 1) * 4 + (y & 1) * 2 + (z & 1)
        source = column * 32 + ((lane >> 6) & 1) * 16 + (lane & 7) * 2 + ((lane >> 5) & 1)
        source = jnp.where(near, source, -1)
        both = code.astype(F32) * 2048.0 + code_l
        kept = [d[0] * inv, d[1] * inv, d[2] * inv, inv, species, source.astype(F32), atom, both]
        for k, value in enumerate(kept):
            pair_buf[pl.ds(at + k, 8, stride=8), :] = value
        return carry

    lax.fori_loop(0, (scatters * SCATTER * TILE + 1023) // 1024, basis, 0)

    for fetch in fetches:
        fetch.wait()
    fi3 = jnp.concatenate([fi_ref[...], jnp.zeros((24, 64), F32)], axis=0)
    si3 = jnp.concatenate([si_ref[...], jnp.zeros((24, 64), F32)], axis=0)

    def inner_weights(padded):
        w = padded.T[:, 0:8]
        high = w.astype(BF16).astype(F32)
        low = w - high
        return jnp.concatenate([high, high, low, jnp.zeros((64, 8), F32)], axis=1).astype(BF16)

    fi_t3 = inner_weights(fi3)
    si_t3 = inner_weights(si3)
    fo_t3 = three_weights(fo_ref[...].T, 1)
    so_t3 = three_weights(so_ref[...].T, 1)
    emb_pad[...] = jnp.zeros((128, 128), F32)
    emb_pad[0:89, :] = emb_ref[...]
    emb_t2 = jnp.concatenate(split(emb_pad[...].T), axis=1)

    def tile_rows(ref, t):
        at = t * 16
        return jnp.concatenate([ref[pl.ds(at, 8), :], ref[pl.ds(at + 8, 8), :]], axis=1)

    def stacked(ref, t):
        rows = tile_rows(ref, t)
        high = rows.astype(BF16).astype(F32)
        stack = jnp.concatenate([high, rows - high, high, jnp.zeros((8, TILE), F32)], axis=0)
        return stack.astype(BF16)

    def radial_of(t, inner, outer):
        hidden, slope = silu_pair(dot(inner, stacked(bes_buf, t)))
        rate = dot(inner, stacked(dbes_buf, t)) * slope
        return dot(outer, three(hidden, 0)), dot(outer, three(rate, 0))

    def onehot(index_row, rows):
        hit = iota((rows, index_row.shape[1]), 0) == index_row.astype(I32)
        return jnp.where(hit, 1.0, 0.0).astype(BF16)

    def sender_of(species_row):
        hot = onehot(species_row, 128)
        return dot(emb_t2, jnp.concatenate([hot, hot], axis=0))

    def first_of(t):
        before = jnp.clip(t - 1, 0, jnp.maximum(tiles - 1, 0))
        return jnp.where(t == 0, 0, last_row[before]) * 2

    acc[...] = jnp.zeros(acc.shape, F32)

    def first_terms(t):
        weights, rates = radial_of(t, fi_t3, fo_t3)
        pair = tile_rows(pair_buf, t)
        sender = sender_of(pair[4:5])
        message = weights[0:128] * sender
        rg = weights[128:256] * sender
        return pair, message, rg, rates[0:128] * sender, rates[128:256] * sender

    def layer_one(step, carry):
        done = []
        for part in range(UNROLL):
            t = step * UNROLL + part
            pair, message, rg, rate_0, rate_1 = first_terms(t)
            kept = jnp.minimum(t, KEPT_TILES)
            saved[kept, 0:128, :] = rg
            saved[kept, 128:256, :] = rate_0
            saved[kept, 256:384, :] = rate_1
            saved_pair_grad[t] = jnp.zeros((8, TILE), F32)
            both = jnp.concatenate(split(message), axis=0), jnp.concatenate(split(rg), axis=0)
            done.append((t, first_of(t) & -8, pair, both))

        def window(entry, w):
            _, base, pair, (m_parts, v_parts) = entry
            at = base + w * WINDOW
            unit = [split(pair[k : k + 1]) for k in range(3)]
            hot = onehot(pair[6:7] - at.astype(F32), WINDOW)
            u_high = jnp.concatenate([hot * high for high, _ in unit], axis=0)
            u_low = jnp.concatenate([hot * low for _, low in unit], axis=0)
            m = dot_t(hot, m_parts)
            v = dot_t(u_high, v_parts)
            m = m[:, 0:128] + m[:, 128:256]
            v = v[:, 0:128] + v[:, 128:256] + dot_t(u_low, v_parts[0:128])
            return pl.ds(pl.multiple_of(at, 8), WINDOW), m, v

        def add(rows, m, v):
            acc[0, rows, :] += m
            for x in range(3):
                acc[1 + x, rows, :] += v[x * WINDOW : (x + 1) * WINDOW]

        for sums in [window(entry, 0) for entry in done]:
            add(*sums)
        counts = [
            jnp.where(t < tiles, (last_row[t] * 2 + 1 - base) // WINDOW + 1, 1)
            for t, base, _, _ in done
        ]
        most = counts[0]
        for count in counts[1:]:
            most = jnp.maximum(most, count)

        @pl.when(most > 1)
        def _():
            for count, entry in zip(counts, done):

                def more(w, carry, entry=entry):
                    add(*window(entry, w))
                    return carry

                lax.fori_loop(1, count, more, 0)

        return carry

    lax.fori_loop(0, steps, layer_one, 0)

    parts = []
    for group in range(4):
        merged = None
        for sub in range(4):
            col = group * 4 + sub
            y, z = COLUMNS[col]
            row, b, c = (y >> 1) * 3 + (z >> 1), y & 1, z & 1
            local = lane8 & 31
            index = ((local >> 4) & 1) * 64 + (local & 1) * 32 + ((local >> 1) & 7) + b * 16 + c * 8
            got = lanes_of(table[3, row], index)
            merged = got if merged is None else jnp.where((lane8 >> 5) == sub, got, merged)
        parts.append(merged)
    species_row = jnp.concatenate(parts, axis=1)[0:1]
    node_t = sender_of(species_row)
    fv_t3 = three_weights(fv_ref[...].T, 1)
    square_t = jnp.zeros((128, 512), F32)
    for x in range(3):
        v3 = three(acc[1 + x, 0:512, :] * 0.25, 1)
        value = dot_t(fv_t3, v3)
        vec_t[x] = value
        square_t = square_t + value * value
        high, low = split(value)
        feat_t[0, 128 + x * 128 : 256 + x * 128, :] = high
        feat_t[1, 128 + x * 128 : 256 + x * 128, :] = low
    fs_t3 = three_weights(fs_ref[...].T, 1)
    fq_t3 = three_weights(fq_ref[...].T, 1)
    pre = dot_t(fs_t3, three(acc[0, 0:512, :] * 0.25, 1))
    pre = pre + dot(fs_t3, three(node_t, 0)) + dot(fq_t3, three(square_t, 0))
    scal_t, slope = silu_pair(pre)
    slope_t[...] = slope
    high, low = split(scal_t)
    feat_t[0, 0:128, :] = high
    feat_t[1, 0:128, :] = low
    scal_core = scal_t[:, 0:128]

    w_acc[...] = jnp.zeros((128, 128), F32)

    def second_terms(t):
        weights, rates = radial_of(t, si_t3, so_t3)
        pair = tile_rows(pair_buf, t)
        hot = onehot(pair[5:6], 512)
        feat = dot(feat_t[...].reshape(1024, 512), hot)
        feat = feat[0:512] + feat[512:1024]
        proj = pair[0:1] * feat[128:256] + pair[1:2] * feat[256:384] + pair[2:3] * feat[384:512]
        rate = rates[0:128] * feat[0:128] + rates[128:256] * proj
        message = weights[0:128] * feat[0:128] + weights[128:256] * proj
        return pair, message, feat[128:512], weights, rate

    def layer_two(t, carry):
        pair, message, vectors, weights, rate = second_terms(t)
        kept = jnp.minimum(t, KEPT_CORE_TILES)
        saved_core[kept, 0:384, :] = vectors
        saved_core[kept, 384:640, :] = weights
        saved_core[kept, 640:768, :] = rate
        high, low = split(message)
        member = onehot(pair[6:7], 128)
        w_acc[...] += dot_t(high, member) + dot_t(low, member)
        return carry

    lax.fori_loop(0, core_tiles, layer_two, 0)

    mixed = w_acc[...] * 0.25 + scal_core
    rs_col = jnp.broadcast_to(rs_ref[...], (128, 128)).T
    rf_col = jnp.broadcast_to(rf_ref[...], (128, 128)).T
    out, out_slope = silu_pair(dot(three_weights(sm_ref[...].T, 1), three(mixed, 0)))
    energy = jnp.sum(out * rs_col + scal_core * rf_col, axis=0, keepdims=True)
    index = (((lane8 >> 3) & 3) * 16 + (lane8 & 7)) * 2 + ((lane8 >> 5) & 1)
    index = jnp.where(lane8 < 64, ((lane8 >> 3) & 3) * 32 + (lane8 & 7) * 2 + ((lane8 >> 5) & 1), 0)
    energy_ref[...] = lanes_of(jnp.broadcast_to(energy, (8, 128)), index)[0:1, 0:64]

    mixed_grad = dot(three_weights(sm_ref[...], 1), three(rs_col * out_slope, 0))
    w_grad2 = jnp.concatenate(split(mixed_grad * 0.25), axis=1)
    feat_grad[...] = jnp.zeros((512, 512), F32)
    feat_grad[0:128, 0:128] = mixed_grad + rf_col

    def layer_two_back(t, carry, again):
        pair = tile_rows(pair_buf, t)
        member = onehot(pair[6:7], 128)
        w_grad = dot(w_grad2, jnp.concatenate([member, member], axis=0))
        if again:
            _, _, vectors, weights, rate = second_terms(t)
        else:
            vectors, weights = saved_core[t, 0:384, :], saved_core[t, 384:640, :]
            rate = saved_core[t, 640:768, :]
        proj_grad = w_grad * weights[128:256]
        grads = [jnp.sum(w_grad * rate, axis=0, keepdims=True)]
        sends = [w_grad * weights[0:128]]
        for x in range(3):
            part = vectors[x * 128 : 128 + x * 128]
            grads.append(jnp.sum(proj_grad * part, axis=0, keepdims=True))
            sends.append(proj_grad * pair[x : x + 1])
        saved_pair_grad[t] = jnp.concatenate(grads + [jnp.zeros((4, TILE), F32)], axis=0)
        high, low = split(jnp.concatenate(sends, axis=0))
        hot = onehot(pair[5:6], 512)
        feat_grad[...] += dot_t(high, hot) + dot_t(low, hot)
        return carry

    kept_core = jnp.minimum(core_tiles, KEPT_CORE_TILES)
    lax.fori_loop(0, kept_core, functools.partial(layer_two_back, again=False), 0)
    lax.fori_loop(kept_core, core_tiles, functools.partial(layer_two_back, again=True), 0)

    pre_grad3 = three(feat_grad[0:128, :] * slope_t[...], 0)
    m_grad = dot(three_weights(fs_ref[...], 1), pre_grad3)
    square_grad = dot(three_weights(fq_ref[...], 1), pre_grad3)
    fv_b3 = three_weights(fv_ref[...], 1)
    message_grads = [m_grad]
    for x in range(3):
        part = feat_grad[128 + x * 128 : 256 + x * 128, :] + 2.0 * vec_t[x] * square_grad
        message_grads.append(dot(fv_b3, three(part, 0)))
    for kind in range(4):
        wide = jnp.concatenate([message_grads[kind] * 0.25, jnp.zeros((128, 128), F32)], axis=1)
        for odd, part in enumerate((wide, pltpu.roll(wide, 576, 1))):
            high, low = split(part)
            for w in range(4):
                rows = pl.ds(kind * 128, 128)
                grad_lhs[2 * w + odd, rows, 0:128] = high[:, w * 128 : (w + 1) * 128]
                grad_lhs[2 * w + odd, rows, 128:256] = low[:, w * 128 : (w + 1) * 128]

    box_acc[...] = jnp.zeros((96, 128), F32)

    def expanded(pair, w):
        member = onehot(pair[6:7] - (w * 64).astype(F32), 128)
        return dot(grad_lhs[w], jnp.concatenate([member, member], axis=0))

    def back_tiles(step, again, many):
        for part in range(UNROLL):
            t = step * UNROLL + part
            pair = tile_rows(pair_buf, t)
            first = first_of(t) >> 6
            moved = expanded(pair, first)
            if many:
                expand[...] = moved
                last = jnp.where(t < tiles, (last_row[t] * 2 + 1) >> 6, 0)

                def more(w, carry, pair=pair, first=first):
                    expand[...] += expanded(pair, first + 2 * w)
                    return carry

                lax.fori_loop(1, ((last - first) >> 1) + 1, more, 0)
                moved = expand[...]
            if again:
                _, _, rg, rate_0, rate_1 = first_terms(t)
            else:
                rg, rate_0, rate_1 = (saved[t, k * 128 : k * 128 + 128, :] for k in range(3))
            earlier = saved_pair_grad[t]
            rho_grad = earlier[0:1] + jnp.sum(moved[0:128] * rate_0, axis=0, keepdims=True)
            unit_grad = []
            for x in range(3):
                v_grad = moved[128 + x * 128 : 256 + x * 128]
                along = jnp.sum(v_grad * rate_1, axis=0, keepdims=True)
                rho_grad = rho_grad + pair[x : x + 1] * along
                across = jnp.sum(v_grad * rg, axis=0, keepdims=True)
                unit_grad.append(across + earlier[1 + x : 2 + x])
            unit = [pair[x : x + 1] for x in range(3)]
            inner = unit[0] * unit_grad[0] + unit[1] * unit_grad[1] + unit[2] * unit_grad[2]
            inv = pair[3:4]
            values = []
            for x in range(3):
                values.append((unit_grad[x] - unit[x] * inner) * inv + rho_grad * unit[x])
            for x in range(3):
                saved_pair_grad[t, x : x + 1, :] = values[x]

    def layer_one_back(step, carry):
        crossing = False
        for part in range(UNROLL):
            t = step * UNROLL + part
            last = jnp.where(t < tiles, (last_row[t] * 2 + 1) >> 6, 0)
            crossing = crossing | (last > (first_of(t) >> 6) + 1)

        @pl.when(crossing)
        def _():
            back_tiles(step, False, True)

        @pl.when(jnp.logical_not(crossing))
        def _():
            back_tiles(step, False, False)

        return carry

    def layer_one_again(step, carry):
        back_tiles(step, True, True)
        return carry

    kept_steps = jnp.minimum(steps, KEPT_TILES // UNROLL)
    lax.fori_loop(0, kept_steps, layer_one_back, 0)
    lax.fori_loop(kept_steps, steps, layer_one_again, 0)

    def scatter(group, carry):
        total_grad = None
        for part in range(SCATTER):
            t = group * SCATTER + part
            pair = tile_rows(pair_buf, t)
            values = []
            for x in range(3):
                value = jnp.where(pair[6:7] >= 0.0, saved_pair_grad[t, x : x + 1, :], 0.0)
                high = value.astype(BF16).astype(F32)
                values += [high, value - high]
            both = pair[7:8].astype(I32)
            rows, lanes = [], []
            for code, sign in ((both >> 11, 1.0), (both & 2047, -1.0)):
                row = jnp.broadcast_to(code >> 7, (16, TILE)) == iota((16, TILE), 0)
                stack = [jnp.where(row, sign * value, 0.0) for value in values]
                rows.append(jnp.concatenate(stack, axis=0).astype(BF16))
                lanes.append(onehot(code & 127, 128))
            moved = dot_t(jnp.concatenate(rows, axis=1), jnp.concatenate(lanes, axis=1))
            total_grad = moved if total_grad is None else total_grad + moved
        box_acc[...] += total_grad
        return carry

    lax.fori_loop(0, scatters, scatter, 0)

    for comp in range(3):
        grid = box_acc[comp * 32 : comp * 32 + 16, :] + box_acc[comp * 32 + 16 : comp * 32 + 32, :]
        for dz, ref in ((-1, down_ref), (0, mid_ref), (1, up_ref)):
            for dy in range(3):
                row = dy * 3 + dz + 1
                ref[dy, comp : comp + 1, :] = grid[row : row + 1, :]
    for ref in (down_ref, mid_ref, up_ref):
        for dy in range(3):
            ref[dy, 3:8, :] = jnp.zeros((5, 128), F32)


def pair_program(own, low, high, weights):
    vm = pltpu.VMEM
    pair_rows = (MAX_TILES * 2 + 6) * 8
    scratch = [
        vm((5, 9, 8, 128), F32),
        vm((256, 128), F32),
        vm((32, 8, 128), F32),
        vm((5, 256, 128), F32),
        vm((256, 128), F32),
        vm((2048, 128), F32),
        vm((pair_rows, 128), F32),
        vm((pair_rows, 128), F32),
        vm((pair_rows, 128), F32),
        vm((pair_rows, 128), F32),
        vm((8, 512), I32),
        pltpu.SMEM((8, 512), I32),
        pltpu.SMEM((256,), I32),
        pltpu.SemaphoreType.DMA,
        vm((4, 512 + WINDOW, 128), F32),
        vm((3, 128, 512), F32),
        vm((128, 512), F32),
        vm((2, 512, 512), BF16),
        vm((512, 512), F32),
        vm((128, 128), F32),
        vm((8, 512, 256), BF16),
        vm((512, TILE), F32),
        vm((KEPT_TILES + 1, 384, TILE), F32),
        vm((KEPT_CORE_TILES + 1, 768, TILE), F32),
        vm((MAX_TILES, 8, TILE), F32),
        vm((96, 128), F32),
        vm((128, 128), F32),
    ]
    scratch += [vm(w.shape, F32) for w in weights]
    scratch.append(pltpu.SemaphoreType.DMA((len(weights),)))
    whole = pl.BlockSpec(memory_space=pltpu.VMEM)
    piece = jax.ShapeDtypeStruct((3, 8, 128), F32)
    return pl.pallas_call(
        main_kernel,
        out_shape=(jax.ShapeDtypeStruct((1, 64), F32), piece, piece, piece),
        in_specs=[whole] * 3 + [pl.BlockSpec(memory_space=pltpu.HBM)] * len(weights),
        out_specs=(whole,) * 4,
        scratch_shapes=scratch,
        compiler_params=pltpu.CompilerParams(vmem_limit_bytes=58 * 1024 * 1024),
        interpret=INTERPRET,
    )(own, low, high, *weights)


def pack(positions, species, counts, neighbors):
    whole = pl.BlockSpec(memory_space=pltpu.VMEM)
    return pl.pallas_call(
        pack_kernel,
        out_shape=jax.ShapeDtypeStruct((5, 8, 128), F32),
        in_specs=[whole] * 4,
        out_specs=whole,
        interpret=INTERPRET,
    )(positions, species.reshape(1, 64), counts.reshape(1, 64), neighbors)


def join_y(own, below, above):
    return jnp.concatenate(
        [below[2:5], below[7:10], own, above[0:2], above[4:7], above[9:10]], axis=0
    )


def ring(axis, step):
    count = lax.axis_size(axis)
    return [(i, (i + step) % count) for i in range(count)]


def shards(
    positions,
    species,
    neighbors,
    neighbor_counts,
    embedding,
    first_inner,
    first_outer,
    first_scalar,
    first_vector,
    first_square,
    second_inner,
    second_outer,
    second_mix,
    readout_first,
    readout_second,
):
    packed = pack(positions, species, neighbor_counts, neighbors)
    partner = lax.ppermute(packed, "gx", ring("gx", 1))
    both = jnp.concatenate([packed, partner], axis=0)
    below = lax.ppermute(both, "gy", ring("gy", 1))
    above = lax.ppermute(both, "gy", ring("gy", -1))
    layer = join_y(both, below, above)
    low = lax.ppermute(layer, "gz", ring("gz", 1))
    high = lax.ppermute(layer, "gz", ring("gz", -1))
    weights = (
        embedding,
        first_inner,
        first_outer,
        first_scalar,
        first_vector,
        first_square,
        second_inner,
        second_outer,
        second_mix,
        readout_first.reshape(1, 128),
        readout_second.reshape(1, 128),
    )
    energy, up, mid, down = pair_program(layer, low, high, weights)
    folded = mid + lax.ppermute(up, "gz", ring("gz", 1)) + lax.ppermute(down, "gz", ring("gz", -1))
    total = folded[1] + lax.ppermute(folded[2], "gy", ring("gy", 1))
    total = total + lax.ppermute(folded[0], "gy", ring("gy", -1))
    return (energy.reshape(64), -total[0:3, 0:64])


def solution(mesh):
    spread = ("gx", "gy", "gz")
    placed = (P(None, spread), P(spread), P(spread, None), P(spread)) + (P(),) * 11
    return jax.shard_map(
        shards,
        mesh=mesh,
        in_specs=placed,
        out_specs=(P(spread), P(None, spread)),
        check_vma=False,
    )
```
